1024 devices in a mesh: grp: 16 (over y, x_lo, core), blk: 64 (over x_hi, z).
Axes of the slice: x: 4 (x_hi: 2, x_lo: 2; x = x_hi * 2 + x_lo), y: 4, z: 32, core: 2. Of those that a mesh axis runs over, the one named last changes fastest.
Arguments:
- adj_tiles: bfloat16 [16384, 256, 256], P(('grp', 'blk')), may hold values from -0.375 to 0.375
- tile_pos: int32 [16384], P(('grp', 'blk')), may hold values from 0 to 255
- tile_count: int32 [1024], P(('grp', 'blk')), may hold values from 1 to 16, as said below
- node_feats: bfloat16 [131072, 128], P(('grp', 'blk')), may hold values from -6 to 6
- stale_part: bfloat16 [16, 16, 8192, 128], P('grp', None, 'blk'), may hold values from -4 to 4
- w_self: bfloat16 [128, 256], replicated, may hold values from -0.5 to 0.5
- w_neigh: bfloat16 [128, 256], replicated, may hold values from -0.25 to 0.25
- bias_vec: float32 [256], replicated, may hold values from -3 to 3
- cotangent: bfloat16 [131072, 256], P(('grp', 'blk')), may hold values from -6 to 6
Outputs:
- new_part: bfloat16 [16, 16, 8192, 128], P('grp', None, 'blk')
- hidden: bfloat16 [131072, 256], P(('grp', 'blk'))
- grad_self: float32 [128, 256], replicated
- grad_neigh: float32 [128, 256], replicated
- grad_bias: float32 [256], replicated
The draws below stay inside these ranges and needn't reach their ends.
Inputs may be any that keep to these rules, and one draw needn't show every extreme that they name: `tile_count`: slots are live only below a device's count; one device has exactly 16 live slots. Tile positions of one device may repeat, and their products then add.
All inputs are finite; a program needn't handle non-finite values.
Results may differ from the reference program's by a relative error of at most 0.019.
Values may be sent and summed in bfloat16 or wider, within the bound.
No kernel may reach another device: no remote copies, remote signals or barrier semaphores. Data moves between devices by JAX's collectives and lax.ppermute only.
A program may use at most 32 MiB of HBM per device.

```python
import jax
import jax.numpy as jnp
from jax import lax

F_IN = 128
HID = 256
TILE = 256
NODE_DEV = 128
TILES_DEV = 16
NODES = 131072
ROW_TILES = 8
COL_TILES = 32
N_GRP = 16
N_BLK = 64


def draw_tile_count(key, part):
    key = jax.random.fold_in(key, 11)
    first_key, second_key = jax.random.split(key)
    devices_all = N_GRP * N_BLK
    raw = jax.random.randint(first_key, (devices_all,), 0, TILES_DEV)
    counts = 1 + raw * raw // TILES_DEV
    busiest = jax.random.randint(second_key, (), 0, devices_all)
    counts = jnp.where(jnp.arange(devices_all) == busiest, TILES_DEV, counts)
    return counts.astype(jnp.int32)


def set_ends(array, own_key, smallest, high):
    place = [jax.random.randint(jax.random.fold_in(own_key, axis), (), 0, length) for axis, length in enumerate(array.shape)]
    main_axis = array.shape.index(max(array.shape))
    neighbour = place[:main_axis] + [(place[main_axis] + 1) % array.shape[main_axis]] + place[main_axis + 1:]
    return array.at[tuple(place)].set(smallest).at[tuple(neighbour)].set(high)


def level_of(own_key, extent, pieces, low, high):
    factor_of = 1.0
    for dim, shards_of in pieces:
        heights = jax.random.uniform(jax.random.fold_in(jax.random.fold_in(own_key, 6), dim), (shards_of,), jnp.float32, low / len(pieces), high / len(pieces))
        factor_of = factor_of * jnp.repeat(jnp.exp(heights), extent[dim] // shards_of).reshape((-1,) + (1,) * (len(extent) - 1 - dim))
    return factor_of


def gaussian(stream_key, dims, spread, most, pieces=(), held_as=jnp.bfloat16):
    factor_of = level_of(stream_key, dims, pieces, -0.22, 0.18) if pieces else 1.0
    result = jax.random.normal(stream_key, dims, jnp.float32) * spread * factor_of
    return jnp.minimum(jnp.maximum(result, -most), most).astype(held_as)


def setup_inputs(seed: int = 0) -> dict:
    arg_keys = jax.random.split(jax.random.key(seed), 10)
    return {
        "adj_tiles": gaussian(arg_keys[0], (N_GRP * N_BLK * TILES_DEV, TILE, TILE), TILE ** -0.5, 0.375, ((0, 1024),)),
        "tile_pos": set_ends(jax.random.randint(arg_keys[1], (N_GRP * N_BLK * TILES_DEV,), 0, ROW_TILES * COL_TILES), jax.random.fold_in(arg_keys[1], 1), 0, (ROW_TILES * COL_TILES) - 1).astype(jnp.int32),
        "tile_count": draw_tile_count(jax.random.fold_in(arg_keys[9], 71), 0),
        "node_feats": gaussian(arg_keys[3], (NODES, F_IN), 1.0, 6.0, ((0, 1024),)),
        "stale_part": gaussian(arg_keys[4], (N_GRP, N_GRP, N_BLK * NODE_DEV, F_IN), 0.5, 4.0, ((0, 16), (2, 64))),
        "w_self": gaussian(arg_keys[5], (F_IN, HID), F_IN ** -0.5, 0.5),
        "w_neigh": gaussian(arg_keys[6], (F_IN, HID), (4 * F_IN) ** -0.5, 0.25),
        "bias_vec": gaussian(arg_keys[7], (HID,), 0.5, 3.0, (), jnp.float32),
        "cotangent": gaussian(arg_keys[8], (NODES, HID), 1.0, 6.0, ((0, 1024),)),
    }


def reference(adj_tiles, tile_pos, tile_count, node_feats, stale_part, w_self, w_neigh, bias_vec, cotangent):
    row_span = N_GRP * NODE_DEV
    col_span = N_BLK * NODE_DEV
    col_tiles = col_span // TILE
    row_tiles = row_span // TILE

    def device_partial(device):
        group = device // N_BLK
        group_rows = lax.dynamic_slice_in_dim(node_feats, (group * col_span).astype(jnp.int32), col_span, 0)
        live_tiles = tile_count[device]

        def add_tile(slot, running):
            flat = (device * TILES_DEV + slot).astype(jnp.int32)
            position = tile_pos[flat]
            row_tile = (position // col_tiles).astype(jnp.int32)
            col_tile = (position % col_tiles).astype(jnp.int32)
            block = lax.dynamic_index_in_dim(adj_tiles, flat, 0, keepdims=False)
            source = lax.dynamic_slice_in_dim(group_rows, (col_tile * TILE).astype(jnp.int32), TILE, 0)
            product = jnp.dot(block, source, preferred_element_type=jnp.float32)
            current = lax.dynamic_index_in_dim(running, row_tile, 0, keepdims=False)
            return lax.dynamic_update_index_in_dim(running, current + product, row_tile, 0)

        start = jnp.zeros((row_tiles, TILE, F_IN), jnp.float32)
        running = lax.fori_loop(jnp.int32(0), live_tiles, add_tile, start)
        partial_rows = running.reshape(N_GRP, NODE_DEV, F_IN)
        own_rows = lax.dynamic_index_in_dim(partial_rows, group.astype(jnp.int32), 0, keepdims=False)
        return partial_rows.astype(jnp.bfloat16), own_rows

    partials, own_fresh = lax.map(device_partial, jnp.arange(N_GRP * N_BLK, dtype=jnp.int32))
    new_part = partials.reshape(N_GRP, N_BLK, N_GRP, NODE_DEV, F_IN).transpose(0, 2, 1, 3, 4)
    new_part = new_part.reshape(N_GRP, N_GRP, N_BLK * NODE_DEV, F_IN)
    keep_mask = (jnp.arange(N_GRP)[:, None] != jnp.arange(N_GRP)[None, :])[:, :, None, None]
    stale_sum = jnp.sum(jnp.where(keep_mask, stale_part.astype(jnp.float32), jnp.float32(0.0)), axis=0)
    stale_sum = stale_sum.reshape(NODES, F_IN)
    aggregate = (own_fresh.reshape(NODES, F_IN) + stale_sum).astype(jnp.bfloat16)
    preact = jnp.dot(node_feats, w_self, preferred_element_type=jnp.float32)
    preact = preact + jnp.dot(aggregate, w_neigh, preferred_element_type=jnp.float32) + bias_vec
    gate = jax.nn.sigmoid(preact)
    hidden = (preact * gate).astype(jnp.bfloat16)
    grad_pre = (cotangent.astype(jnp.float32) * gate * (1.0 + preact * (1.0 - gate))).astype(jnp.bfloat16)
    scaling = float(NODES) ** -0.5
    grad_self = jnp.dot(node_feats.T, grad_pre, preferred_element_type=jnp.float32) * scaling
    grad_neigh = jnp.dot(aggregate.T, grad_pre, preferred_element_type=jnp.float32) * scaling
    grad_bias = jnp.sum(grad_pre.astype(jnp.float32), axis=0) * scaling
    return (new_part, hidden, grad_self, grad_neigh, grad_bias)
```

```python
import functools

import jax
import jax.numpy as jnp
from jax import lax
from jax.experimental import pallas as pl
from jax.experimental.pallas import tpu as pltpu
from jax.sharding import Mesh, PartitionSpec as P

GRP = ("y", "x_lo", "core")
PLANE = ("y", "x_lo", "core", "x_hi")
BLK = ("x_hi", "z_far", "z_near")
ALL = GRP + BLK
SIZES = (4, 2, 2, 2, 8, 4)


def spread(value, axes):
    copies = lax.axis_size(axes)
    return lax.all_to_all(
        jnp.broadcast_to(value[None], (copies,) + value.shape), axes, 0, 0, tiled=True
    )


def layer_kernel(
    count_ref,
    pos_ref,
    place_ref,
    own_ref,
    adj_ref,
    rows_ref,
    stale_ref,
    feats_ref,
    w_self_ref,
    w_neigh_ref,
    bias_ref,
    cot_ref,
    part_ref,
    hidden_ref,
    grads_ref,
    acc_ref,
):
    tile = adj_ref.shape[1]
    groups, node_dev, width = part_ref.shape
    per_tile = tile // node_dev
    col_tiles = rows_ref.shape[0] // per_tile
    own = own_ref[0]
    acc_ref[...] = jnp.zeros_like(acc_ref)

    def add_tile(slot, carry):
        position = pos_ref[slot]
        row_tile = lax.div(position, col_tiles)
        first = lax.rem(position, col_tiles) * per_tile
        source = jnp.concatenate(
            [rows_ref[place_ref[first + j]] for j in range(per_tile)], axis=0
        )
        product = jnp.dot(adj_ref[slot], source, preferred_element_type=jnp.float32)
        rows = pl.ds(pl.multiple_of(row_tile * tile, tile), tile)
        acc_ref[rows, :] += product
        return carry

    lax.fori_loop(0, count_ref[0], add_tile, 0)
    part_ref[...] = acc_ref[...].reshape(part_ref.shape).astype(part_ref.dtype)
    total = acc_ref[pl.ds(pl.multiple_of(own * node_dev, node_dev), node_dev), :]
    stale = jnp.zeros((node_dev, width), jnp.float32)
    for source in range(groups):
        keep = jnp.where(source == own, jnp.float32(0.0), jnp.float32(1.0))
        stale += stale_ref[source].astype(jnp.float32) * keep
    aggregate = (total + stale).astype(jnp.bfloat16)
    feats = feats_ref[...]
    preact = jnp.dot(feats, w_self_ref[...], preferred_element_type=jnp.float32)
    preact += jnp.dot(aggregate, w_neigh_ref[...], preferred_element_type=jnp.float32)
    preact += bias_ref[...]
    gate = jax.nn.sigmoid(preact)
    hidden_ref[...] = (preact * gate).astype(hidden_ref.dtype)
    grad_pre = (
        cot_ref[...].astype(jnp.float32) * gate * (1.0 + preact * (1.0 - gate))
    ).astype(jnp.bfloat16)
    both = jnp.concatenate([feats, aggregate], axis=1)
    grads = lax.dot_general(
        both, grad_pre, (((0,), (0,)), ((), ())), preferred_element_type=jnp.float32
    )
    bias_grad = jnp.sum(grad_pre.astype(jnp.float32), axis=0, keepdims=True)
    pieces, piece_rows, _ = grads_ref.shape
    hid = grads.shape[1]
    grads_ref[:, :, :hid] = grads.reshape(pieces, piece_rows, hid)
    half = hid // 2
    tail = jnp.concatenate(
        [
            bias_grad[:, :half],
            bias_grad[:, half:],
            jnp.zeros((piece_rows - 2, half), jnp.float32),
        ],
        axis=0,
    )
    grads_ref[:, :, hid:] = jnp.broadcast_to(tail[None], (pieces, piece_rows, half))


def body(
    adj_tiles, tile_pos, tile_count, node_feats, stale_part, w_self, w_neigh, bias_vec, cotangent
):
    node_dev, width = node_feats.shape
    hid = cotangent.shape[1]
    groups = lax.axis_size(GRP)
    blocks = lax.axis_size(BLK)
    plane = lax.axis_size(PLANE)
    far, near, sides = SIZES[4], SIZES[5], SIZES[3]

    stale = lax.all_to_all(stale_part[0], GRP, 0, 0, tiled=True)
    rows = spread(node_feats, "z_far")
    rows = spread(rows, "z_near")
    rows = spread(rows, "x_hi").reshape(blocks, node_dev, width)
    index = jnp.arange(blocks, dtype=jnp.int32)
    side, line = index // (far * near), index % (far * near)
    place = side * (far * near) + (line % near) * far + line // near
    own = lax.axis_index(GRP).reshape(1).astype(jnp.int32)

    smem = pl.BlockSpec(memory_space=pltpu.SMEM)
    vmem = pl.BlockSpec(memory_space=pltpu.VMEM)
    piece_rows = 2 * width // plane
    new_part, hidden, grads = pl.pallas_call(
        layer_kernel,
        out_shape=(
            jax.ShapeDtypeStruct((groups, node_dev, width), jnp.bfloat16),
            jax.ShapeDtypeStruct((node_dev, hid), jnp.bfloat16),
            jax.ShapeDtypeStruct((plane, piece_rows, hid + hid // 2), jnp.float32),
        ),
        in_specs=[smem] * 4 + [vmem] * 8,
        out_specs=(vmem, vmem, vmem),
        scratch_shapes=[pltpu.VMEM((groups * node_dev, width), jnp.float32)],
        compiler_params=pltpu.CompilerParams(vmem_limit_bytes=32 * 1024 * 1024),
    )(
        tile_count,
        tile_pos,
        place,
        own,
        adj_tiles,
        rows,
        stale,
        node_feats,
        w_self,
        w_neigh,
        bias_vec[None],
        cotangent,
    )

    scaling = float(node_dev * groups * blocks) ** (-0.5)
    piece = jnp.sum(lax.all_to_all(grads, PLANE, 0, 0, tiled=True), axis=0)
    piece = jnp.sum(spread(piece, "z_far"), axis=0)
    piece = jnp.sum(spread(piece, "z_near"), axis=0) * scaling
    grad_bias = piece[:2, hid:].reshape(hid)
    whole = spread(piece[:, :hid], PLANE).reshape(2 * width, hid)
    return new_part[None], hidden, whole[:width], whole[width:], grad_bias


def solution(mesh):
    fine = Mesh(mesh.devices.reshape(SIZES), ALL)
    placed = (
        P(ALL, None, None),
        P(ALL),
        P(ALL),
        P(ALL, None),
        P(GRP, None, BLK, None),
        P(),
        P(),
        P(),
        P(ALL, None),
    )
    return jax.shard_map(
        body,
        mesh=fine,
        in_specs=placed,
        out_specs=(P(GRP, None, BLK, None), P(ALL, None), P(), P(), P()),
        check_vma=False,
    )
```

```python
import functools

import jax
import jax.numpy as jnp
from jax import lax
from jax.experimental import pallas as pl
from jax.experimental.pallas import tpu as pltpu
from jax.sharding import Mesh, PartitionSpec as P

GRP = ("y", "x_lo", "core")
PLANE = ("y", "x_lo", "core", "x_hi")
LINE = ("z_far", "z_mid", "z_near")
EVERY_OTHER = ("z_far", "z_mid")
BLK = ("x_hi",) + LINE
ALL = GRP + BLK
SIZES = (4, 2, 2, 2, 8, 2, 2)


def spread(value, axes):
    copies = lax.axis_size(axes)
    return lax.all_to_all(
        jnp.broadcast_to(value[None], (copies,) + value.shape), axes, 0, 0, tiled=True
    )


def layer_kernel(
    count_ref,
    pos_ref,
    place_ref,
    own_ref,
    adj_ref,
    same_ref,
    left_ref,
    right_ref,
    side_ref,
    side_left_ref,
    side_right_ref,
    stale_ref,
    feats_ref,
    w_self_ref,
    w_neigh_ref,
    bias_ref,
    cot_ref,
    part_ref,
    hidden_ref,
    grads_ref,
    acc_ref,
    source_ref,
):
    tile = adj_ref.shape[1]
    groups, node_dev, width = part_ref.shape
    per_tile = tile // node_dev
    banks = (same_ref, left_ref, right_ref, side_ref, side_left_ref, side_right_ref)
    slots = same_ref.shape[0]
    col_tiles = place_ref.shape[0] // per_tile
    own = own_ref[0]
    acc_ref[...] = jnp.zeros_like(acc_ref)

    def add_tile(slot, carry):
        position = pos_ref[slot]
        row_tile = lax.div(position, col_tiles)
        first = lax.rem(position, col_tiles) * per_tile
        for j in range(per_tile):
            place = place_ref[first + j]
            bank, block = lax.div(place, slots), lax.rem(place, slots)
            for choice, ref in enumerate(banks):

                @pl.when(bank == choice)
                def _():
                    source_ref[j * node_dev : (j + 1) * node_dev, :] = ref[block]

        product = jnp.dot(adj_ref[slot], source_ref[...], preferred_element_type=jnp.float32)
        rows = pl.ds(pl.multiple_of(row_tile * tile, tile), tile)
        acc_ref[rows, :] += product
        return carry

    lax.fori_loop(0, count_ref[0], add_tile, 0)
    part_ref[...] = acc_ref[...].reshape(part_ref.shape).astype(part_ref.dtype)
    total = acc_ref[pl.ds(pl.multiple_of(own * node_dev, node_dev), node_dev), :]
    stale = jnp.zeros((node_dev, width), jnp.float32)
    for source in range(groups):
        keep = jnp.where(source == own, jnp.float32(0.0), jnp.float32(1.0))
        stale += stale_ref[source].astype(jnp.float32) * keep
    aggregate = (total + stale).astype(jnp.bfloat16)
    feats = feats_ref[...]
    preact = jnp.dot(feats, w_self_ref[...], preferred_element_type=jnp.float32)
    preact += jnp.dot(aggregate, w_neigh_ref[...], preferred_element_type=jnp.float32)
    preact += bias_ref[...]
    gate = jax.nn.sigmoid(preact)
    hidden_ref[...] = (preact * gate).astype(hidden_ref.dtype)
    grad_pre = (
        cot_ref[...].astype(jnp.float32) * gate * (1.0 + preact * (1.0 - gate))
    ).astype(jnp.bfloat16)
    both = jnp.concatenate([feats, aggregate], axis=1)
    grads = lax.dot_general(
        both, grad_pre, (((0,), (0,)), ((), ())), preferred_element_type=jnp.float32
    )
    bias_grad = jnp.sum(grad_pre.astype(jnp.float32), axis=0, keepdims=True)
    pieces, piece_rows, _ = grads_ref.shape
    hid = grads.shape[1]
    grads_ref[:, :, :hid] = grads.reshape(pieces, piece_rows, hid)
    half = hid // 2
    tail = jnp.concatenate(
        [
            bias_grad[:, :half],
            bias_grad[:, half:],
            jnp.zeros((piece_rows - 2, half), jnp.float32),
        ],
        axis=0,
    )
    grads_ref[:, :, hid:] = jnp.broadcast_to(tail[None], (pieces, piece_rows, half))


def body(
    adj_tiles, tile_pos, tile_count, node_feats, stale_part, w_self, w_neigh, bias_vec, cotangent
):
    node_dev, width = node_feats.shape
    hid = cotangent.shape[1]
    groups = lax.axis_size(GRP)
    blocks = lax.axis_size(BLK)
    plane = lax.axis_size(PLANE)

    stale = lax.all_to_all(stale_part[0], GRP, 0, 0, tiled=True)
    same = lax.all_gather(node_feats, EVERY_OTHER)
    length = lax.axis_size(LINE)
    up = [(i, (i + 1) % length) for i in range(length)]
    down = [(i, (i - 1) % length) for i in range(length)]
    half = same.shape[0] // 2
    side = lax.ppermute(same, "x_hi", [(0, 1), (1, 0)])
    banks = (
        same,
        lax.ppermute(same[:half], LINE, up),
        lax.ppermute(same[half:], LINE, down),
        side,
        lax.ppermute(side[:half], LINE, up),
        lax.ppermute(side[half:], LINE, down),
    )
    index = jnp.arange(blocks, dtype=jnp.int32)
    other_side = index // length != lax.axis_index("x_hi")
    other_parity = index % 2 != lax.axis_index("z_near")
    slot = index % length // 2
    slots = 2 * half
    across = jnp.where(slot < half, slots + slot, 2 * slots + slot - half)
    place = jnp.where(other_parity, across, slot) + jnp.where(other_side, 3 * slots, 0)
    own = lax.axis_index(GRP).reshape(1).astype(jnp.int32)

    smem = pl.BlockSpec(memory_space=pltpu.SMEM)
    vmem = pl.BlockSpec(memory_space=pltpu.VMEM)
    piece_rows = 2 * width // plane
    new_part, hidden, grads = pl.pallas_call(
        layer_kernel,
        out_shape=(
            jax.ShapeDtypeStruct((groups, node_dev, width), jnp.bfloat16),
            jax.ShapeDtypeStruct((node_dev, hid), jnp.bfloat16),
            jax.ShapeDtypeStruct((plane, piece_rows, hid + hid // 2), jnp.float32),
        ),
        in_specs=[smem] * 4 + [vmem] * 13,
        out_specs=(vmem, vmem, vmem),
        scratch_shapes=[
            pltpu.VMEM((groups * node_dev, width), jnp.float32),
            pltpu.VMEM((adj_tiles.shape[1], width), jnp.bfloat16),
        ],
        compiler_params=pltpu.CompilerParams(vmem_limit_bytes=32 * 1024 * 1024),
    )(
        tile_count,
        tile_pos,
        place,
        own,
        adj_tiles,
        *banks,
        stale,
        node_feats,
        w_self,
        w_neigh,
        bias_vec[None],
        cotangent,
    )

    scaling = float(node_dev * groups * blocks) ** (-0.5)
    piece = jnp.sum(lax.all_to_all(grads, PLANE, 0, 0, tiled=True), axis=0)
    piece = spread(piece.astype(jnp.bfloat16), "z_far")
    piece = jnp.sum(piece.astype(jnp.float32), axis=0)
    piece = jnp.sum(spread(piece, ("z_mid", "z_near")), axis=0) * scaling
    grad_bias = piece[:2, hid:].reshape(hid)
    whole = spread(piece[:, :hid], PLANE).reshape(2 * width, hid)
    return new_part[None], hidden, whole[:width], whole[width:], grad_bias


def solution(mesh):
    fine = Mesh(mesh.devices.reshape(SIZES), ALL)
    placed = (
        P(ALL, None, None),
        P(ALL),
        P(ALL),
        P(ALL, None),
        P(GRP, None, BLK, None),
        P(),
        P(),
        P(),
        P(ALL, None),
    )
    return jax.shard_map(
        body,
        mesh=fine,
        in_specs=placed,
        out_specs=(P(GRP, None, BLK, None), P(ALL, None), P(), P(), P()),
        check_vma=False,
    )
```

```python
import jax
import jax.numpy as jnp
from jax import lax
from jax.experimental import pallas as pl
from jax.experimental.pallas import tpu as pltpu
from jax.sharding import Mesh, PartitionSpec as P

GRP = ("y", "x_lo", "core")
PLANE = ("y", "x_lo", "core", "x_hi")
LINE = ("z_far", "z_mid", "z_near")
EVERY_OTHER = ("z_far", "z_mid")
BLK = ("x_hi",) + LINE
ALL = GRP + BLK
SIZES = (4, 2, 2, 2, 8, 2, 2)


def spread(value, axes):
    copies = lax.axis_size(axes)
    return lax.all_to_all(
        jnp.broadcast_to(value[None], (copies,) + value.shape), axes, 0, 0, tiled=True
    )


def split_position(position, col_tiles, per_tile):
    return lax.div(position, col_tiles), lax.rem(position, col_tiles) * per_tile


def layer_kernel(
    count_ref,
    pos_ref,
    place_ref,
    own_ref,
    adj_ref,
    bank_refs,
    stale_ref,
    feats_ref,
    w_self_ref,
    w_neigh_ref,
    bias_ref,
    cot_ref,
    hidden_ref,
    grads_ref,
    pos_out_ref,
    tiles_ref,
    sources_ref,
    stale_vmem,
    feats_vmem,
    w_self_vmem,
    w_neigh_vmem,
    cot_vmem,
    tile_sem,
    source_sem,
    dense_sem,
):
    tile = adj_ref.shape[1]
    groups, node_dev, width = stale_ref.shape
    per_tile = tile // node_dev
    bank_slots = bank_refs[0].shape[0]
    col_tiles = place_ref.shape[0] // per_tile
    own = own_ref[0]
    own_tile, own_part = lax.div(own, per_tile), lax.rem(own, per_tile)
    count = count_ref[0]

    dense = [
        pltpu.make_async_copy(src, dst, dense_sem.at[i])
        for i, (src, dst) in enumerate(
            (
                (stale_ref, stale_vmem),
                (feats_ref, feats_vmem),
                (w_self_ref, w_self_vmem),
                (w_neigh_ref, w_neigh_vmem),
                (cot_ref, cot_vmem),
            )
        )
    ]

    def tile_copy(slot):
        rows = pl.ds(pl.multiple_of(own_part * node_dev, node_dev), node_dev)
        return pltpu.make_async_copy(
            adj_ref.at[slot, rows, :], tiles_ref.at[slot], tile_sem.at[slot]
        )

    def source_copy(slot, j, bank, block):
        return pltpu.make_async_copy(
            bank.at[block],
            sources_ref.at[slot, pl.ds(j * node_dev, node_dev), :],
            source_sem.at[slot, j],
        )

    def fetch(slot, carry):
        pos_out_ref[slot] = pos_ref[slot]
        row_tile, first = split_position(pos_ref[slot], col_tiles, per_tile)

        @pl.when((row_tile == own_tile) & (slot < count))
        def _():
            tile_copy(slot).start()
            for j in range(per_tile):
                place = place_ref[first + j]
                bank, block = lax.div(place, bank_slots), lax.rem(place, bank_slots)
                for choice, ref in enumerate(bank_refs):

                    @pl.when(bank == choice)
                    def _():
                        source_copy(slot, j, ref, block).start()

        return carry

    lax.fori_loop(0, pos_ref.shape[0], fetch, 0)
    for copy in dense:
        copy.start()

    def add_tile(slot, fresh):
        row_tile, _ = split_position(pos_ref[slot], col_tiles, per_tile)

        def add():
            tile_copy(slot).wait()
            for j in range(per_tile):
                source_copy(slot, j, bank_refs[0], 0).wait()
            return fresh + jnp.dot(
                tiles_ref[slot], sources_ref[slot], preferred_element_type=jnp.float32
            )

        return lax.cond(row_tile == own_tile, add, lambda: fresh)

    fresh = lax.fori_loop(0, count, add_tile, jnp.zeros((node_dev, width), jnp.float32))
    for copy in dense:
        copy.wait()
    stale = jnp.zeros((node_dev, width), jnp.float32)
    for source in range(groups):
        keep = jnp.where(source == own, jnp.float32(0.0), jnp.float32(1.0))
        stale += stale_vmem[source].astype(jnp.float32) * keep
    aggregate = (fresh + stale).astype(jnp.bfloat16)
    feats = feats_vmem[...]
    preact = jnp.dot(feats, w_self_vmem[...], preferred_element_type=jnp.float32)
    preact += jnp.dot(aggregate, w_neigh_vmem[...], preferred_element_type=jnp.float32)
    preact += bias_ref[...]
    gate = jax.nn.sigmoid(preact)
    hidden_ref[...] = (preact * gate).astype(hidden_ref.dtype)
    grad_pre = (
        cot_vmem[...].astype(jnp.float32) * gate * (1.0 + preact * (1.0 - gate))
    ).astype(jnp.bfloat16)
    both = jnp.concatenate([feats, aggregate], axis=1)
    grads = lax.dot_general(
        both, grad_pre, (((0,), (0,)), ((), ())), preferred_element_type=jnp.float32
    )
    bias_grad = jnp.sum(grad_pre.astype(jnp.float32), axis=0, keepdims=True)
    pieces, piece_rows, _ = grads_ref.shape
    hid = grads.shape[1]
    grads_ref[:, :, :hid] = grads.reshape(pieces, piece_rows, hid).astype(grads_ref.dtype)
    half = hid // 2
    tail = jnp.concatenate(
        [
            bias_grad[:, :half],
            bias_grad[:, half:],
            jnp.zeros((piece_rows - 2, half), jnp.float32),
        ],
        axis=0,
    )
    grads_ref[:, :, hid:] = jnp.broadcast_to(tail[None], (pieces, piece_rows, half)).astype(
        grads_ref.dtype
    )


def partial_kernel(
    count_ref, pos_ref, place_ref, adj_ref, bank_refs, part_ref, acc_ref, source_ref
):
    tile = adj_ref.shape[1]
    _, node_dev, _ = part_ref.shape
    per_tile = tile // node_dev
    bank_slots = bank_refs[0].shape[0]
    col_tiles = place_ref.shape[0] // per_tile
    acc_ref[...] = jnp.zeros_like(acc_ref)

    def add_tile(slot, carry):
        row_tile, first = split_position(pos_ref[slot], col_tiles, per_tile)
        for j in range(per_tile):
            place = place_ref[first + j]
            bank, block = lax.div(place, bank_slots), lax.rem(place, bank_slots)
            for choice, ref in enumerate(bank_refs):

                @pl.when(bank == choice)
                def _():
                    source_ref[j * node_dev : (j + 1) * node_dev, :] = ref[block]

        product = jnp.dot(adj_ref[slot], source_ref[...], preferred_element_type=jnp.float32)
        rows = pl.ds(pl.multiple_of(row_tile * tile, tile), tile)
        acc_ref[rows, :] += product
        return carry

    lax.fori_loop(0, count_ref[0], add_tile, 0)
    part_ref[...] = acc_ref[...].reshape(part_ref.shape).astype(part_ref.dtype)


def body(
    adj_tiles, tile_pos, tile_count, node_feats, stale_part, w_self, w_neigh, bias_vec, cotangent
):
    node_dev, width = node_feats.shape
    hid = cotangent.shape[1]
    groups = lax.axis_size(GRP)
    blocks = lax.axis_size(BLK)
    plane = lax.axis_size(PLANE)

    stale = lax.all_to_all(stale_part[0], GRP, 0, 0, tiled=True)
    same = lax.all_gather(node_feats, EVERY_OTHER)
    length = lax.axis_size(LINE)
    up = [(i, (i + 1) % length) for i in range(length)]
    down = [(i, (i - 1) % length) for i in range(length)]
    half = same.shape[0] // 2
    low, high = same[:half], same[half:]
    swap = [(0, 1), (1, 0)]
    side_low, side_high = lax.ppermute(low, "x_hi", swap), lax.ppermute(high, "x_hi", swap)
    banks = (
        low,
        high,
        lax.ppermute(low, LINE, up),
        lax.ppermute(high, LINE, down),
        side_low,
        side_high,
        lax.ppermute(side_low, LINE, up),
        lax.ppermute(side_high, LINE, down),
    )
    index = jnp.arange(blocks, dtype=jnp.int32)
    other_side = index // length != lax.axis_index("x_hi")
    other_parity = index % 2 != lax.axis_index("z_near")
    slot = index % length // 2
    place = slot + length // 2 * (other_parity.astype(jnp.int32) + 2 * other_side)
    own = lax.axis_index(GRP).reshape(1).astype(jnp.int32)

    smem = pl.BlockSpec(memory_space=pltpu.SMEM)
    vmem = pl.BlockSpec(memory_space=pltpu.VMEM)
    piece_rows = 2 * width // plane
    tile, slots = adj_tiles.shape[1], adj_tiles.shape[0]
    whole = pl.BlockSpec(memory_space=pl.ANY)
    bf16, f32 = jnp.bfloat16, jnp.float32
    limit = pltpu.CompilerParams(vmem_limit_bytes=32 * 1024 * 1024)
    hidden, grads, positions = pl.pallas_call(
        layer_kernel,
        out_shape=(
            jax.ShapeDtypeStruct((node_dev, hid), bf16),
            jax.ShapeDtypeStruct((plane, piece_rows, hid + hid // 2), bf16),
            jax.ShapeDtypeStruct(tile_pos.shape, jnp.int32),
        ),
        in_specs=[smem] * 4 + [whole, [whole] * len(banks)] + [whole] * 4 + [vmem, whole],
        out_specs=(vmem, vmem, smem),
        scratch_shapes=[
            pltpu.VMEM((slots, node_dev, tile), bf16),
            pltpu.VMEM((slots, tile, width), bf16),
            pltpu.VMEM((groups, node_dev, width), bf16),
            pltpu.VMEM((node_dev, width), bf16),
            pltpu.VMEM((width, hid), bf16),
            pltpu.VMEM((width, hid), bf16),
            pltpu.VMEM((node_dev, hid), bf16),
            pltpu.SemaphoreType.DMA((slots,)),
            pltpu.SemaphoreType.DMA((slots, tile // node_dev)),
            pltpu.SemaphoreType.DMA((5,)),
        ],
        compiler_params=limit,
        cost_estimate=pl.CostEstimate(
            flops=10 * node_dev * width * hid, bytes_accessed=2**20, transcendentals=0
        ),
    )(
        tile_count,
        tile_pos,
        place,
        own,
        adj_tiles,
        list(banks),
        stale,
        node_feats,
        w_self,
        w_neigh,
        bias_vec[None],
        cotangent,
    )
    new_part = pl.pallas_call(
        partial_kernel,
        out_shape=jax.ShapeDtypeStruct((groups, node_dev, width), bf16),
        in_specs=[smem] * 3 + [vmem, [vmem] * len(banks)],
        out_specs=vmem,
        scratch_shapes=[
            pltpu.VMEM((groups * node_dev, width), f32),
            pltpu.VMEM((tile, width), bf16),
        ],
        compiler_params=limit,
        cost_estimate=pl.CostEstimate(
            flops=2 * slots * tile * tile * width, bytes_accessed=8 * 2**20, transcendentals=0
        ),
    )(tile_count, positions, place, adj_tiles, list(banks))

    scaling = float(node_dev * groups * blocks) ** (-0.5)
    piece = lax.all_to_all(grads, PLANE, 0, 0, tiled=True).astype(f32)
    piece = spread(jnp.sum(piece, axis=0).astype(bf16), "z_far").astype(f32)
    piece = jnp.sum(spread(jnp.sum(piece, axis=0), ("z_mid", "z_near")), axis=0) * scaling
    grad_bias = piece[:2, hid:].reshape(hid)
    both = spread(piece[:, :hid].astype(bf16), PLANE).astype(f32).reshape(2 * width, hid)
    return new_part[None], hidden, both[:width], both[width:], grad_bias


def solution(mesh):
    fine = Mesh(mesh.devices.reshape(SIZES), ALL)
    placed = (
        P(ALL, None, None),
        P(ALL),
        P(ALL),
        P(ALL, None),
        P(GRP, None, BLK, None),
        P(),
        P(),
        P(),
        P(ALL, None),
    )
    return jax.shard_map(
        body,
        mesh=fine,
        in_specs=placed,
        out_specs=(P(GRP, None, BLK, None), P(ALL, None), P(), P(), P()),
        check_vma=False,
    )
```

```python
import jax
import jax.numpy as jnp
from jax import lax
from jax.experimental import pallas as pl
from jax.experimental.pallas import tpu as pltpu
from jax.sharding import Mesh, PartitionSpec as P

GRP = ("y", "x_lo", "core")
PLANE = ("y", "x_lo", "core", "x_hi")
LINE = ("z_far", "z_mid", "z_near")
EVERY_OTHER = ("z_far", "z_mid")
BLK = ("x_hi",) + LINE
ALL = GRP + BLK
SIZES = (4, 2, 2, 2, 8, 2, 2)


def spread(value, axes):
    copies = lax.axis_size(axes)
    return lax.all_to_all(
        jnp.broadcast_to(value[None], (copies,) + value.shape), axes, 0, 0, tiled=True
    )


def split_position(position, col_tiles, per_tile):
    return lax.div(position, col_tiles), lax.rem(position, col_tiles) * per_tile


def early_kernel(
    own_ref, stale_ref, feats_ref, w_self_ref, w_neigh_ref, cot_ref,
    sum_ref, base_ref, w_neigh_out, cot_out,
):
    groups = stale_ref.shape[0]
    own = own_ref[0]
    stale = jnp.zeros(sum_ref.shape, jnp.float32)
    for source in range(groups):
        keep = jnp.where(source == own, jnp.float32(0.0), jnp.float32(1.0))
        stale += stale_ref[source].astype(jnp.float32) * keep
    sum_ref[...] = stale
    preact = jnp.dot(feats_ref[...], w_self_ref[...], preferred_element_type=jnp.float32)
    base_ref[...] = preact
    w_neigh_out[...] = w_neigh_ref[...]
    cot_out[...] = cot_ref[...]


def layer_kernel(
    count_ref,
    pos_ref,
    place_ref,
    own_ref,
    adj_ref,
    bank_refs,
    stale_ref,
    base_ref,
    feats_ref,
    w_neigh_ref,
    bias_ref,
    cot_ref,
    hidden_ref,
    grads_ref,
    pos_out_ref,
    tiles_ref,
    sources_ref,
    tile_sem,
    source_sem,
):
    tile = adj_ref.shape[1]
    node_dev, width = stale_ref.shape
    per_tile = tile // node_dev
    bank_slots = bank_refs[0].shape[0]
    col_tiles = place_ref.shape[0] // per_tile
    own = own_ref[0]
    own_tile, own_part = lax.div(own, per_tile), lax.rem(own, per_tile)
    count = count_ref[0]

    def tile_copy(slot):
        rows = pl.ds(pl.multiple_of(own_part * node_dev, node_dev), node_dev)
        return pltpu.make_async_copy(
            adj_ref.at[slot, rows, :], tiles_ref.at[slot], tile_sem.at[slot]
        )

    def source_copy(slot, j, bank, block):
        return pltpu.make_async_copy(
            bank.at[block],
            sources_ref.at[slot, pl.ds(j * node_dev, node_dev), :],
            source_sem.at[slot, j],
        )

    def fetch(slot, carry):
        pos_out_ref[slot] = pos_ref[slot]
        row_tile, first = split_position(pos_ref[slot], col_tiles, per_tile)

        @pl.when((row_tile == own_tile) & (slot < count))
        def _():
            tile_copy(slot).start()
            for j in range(per_tile):
                place = place_ref[first + j]
                bank, block = lax.div(place, bank_slots), lax.rem(place, bank_slots)
                for choice, ref in enumerate(bank_refs):

                    @pl.when(bank == choice)
                    def _():
                        source_copy(slot, j, ref, block).start()

        return carry

    lax.fori_loop(0, pos_ref.shape[0], fetch, 0)

    def add_tile(slot, fresh):
        row_tile, _ = split_position(pos_ref[slot], col_tiles, per_tile)

        def add():
            tile_copy(slot).wait()
            for j in range(per_tile):
                source_copy(slot, j, bank_refs[0], 0).wait()
            return fresh + jnp.dot(
                tiles_ref[slot], sources_ref[slot], preferred_element_type=jnp.float32
            )

        return lax.cond(row_tile == own_tile, add, lambda: fresh)

    fresh = lax.fori_loop(0, count, add_tile, jnp.zeros((node_dev, width), jnp.float32))
    aggregate = (fresh + stale_ref[...]).astype(jnp.bfloat16)
    feats = feats_ref[...]
    preact = base_ref[...]
    preact += jnp.dot(aggregate, w_neigh_ref[...], preferred_element_type=jnp.float32)
    preact += bias_ref[...]
    gate = jax.nn.sigmoid(preact)
    hidden_ref[...] = (preact * gate).astype(hidden_ref.dtype)
    grad_pre = (
        cot_ref[...].astype(jnp.float32) * gate * (1.0 + preact * (1.0 - gate))
    ).astype(jnp.bfloat16)
    both = jnp.concatenate([feats, aggregate], axis=1)
    grads = lax.dot_general(
        both, grad_pre, (((0,), (0,)), ((), ())), preferred_element_type=jnp.float32
    )
    bias_grad = jnp.sum(grad_pre.astype(jnp.float32), axis=0, keepdims=True)
    pieces, piece_rows, _ = grads_ref.shape
    hid = grads.shape[1]
    grads_ref[:, :, :hid] = grads.reshape(pieces, piece_rows, hid).astype(grads_ref.dtype)
    half = hid // 2
    tail = jnp.concatenate(
        [
            bias_grad[:, :half],
            bias_grad[:, half:],
            jnp.zeros((piece_rows - 2, half), jnp.float32),
        ],
        axis=0,
    )
    grads_ref[:, :, hid:] = jnp.broadcast_to(tail[None], (pieces, piece_rows, half)).astype(
        grads_ref.dtype
    )


def partial_kernel(
    count_ref, pos_ref, place_ref, adj_ref, bank_refs, part_ref, acc_ref, source_ref
):
    tile = adj_ref.shape[1]
    _, node_dev, _ = part_ref.shape
    per_tile = tile // node_dev
    bank_slots = bank_refs[0].shape[0]
    col_tiles = place_ref.shape[0] // per_tile
    acc_ref[...] = jnp.zeros_like(acc_ref)

    def add_tile(slot, carry):
        row_tile, first = split_position(pos_ref[slot], col_tiles, per_tile)
        for j in range(per_tile):
            place = place_ref[first + j]
            bank, block = lax.div(place, bank_slots), lax.rem(place, bank_slots)
            for choice, ref in enumerate(bank_refs):

                @pl.when(bank == choice)
                def _():
                    source_ref[j * node_dev : (j + 1) * node_dev, :] = ref[block]

        product = jnp.dot(adj_ref[slot], source_ref[...], preferred_element_type=jnp.float32)
        rows = pl.ds(pl.multiple_of(row_tile * tile, tile), tile)
        acc_ref[rows, :] += product
        return carry

    lax.fori_loop(0, count_ref[0], add_tile, 0)
    part_ref[...] = acc_ref[...].reshape(part_ref.shape).astype(part_ref.dtype)


def body(
    adj_tiles, tile_pos, tile_count, node_feats, stale_part, w_self, w_neigh, bias_vec, cotangent
):
    node_dev, width = node_feats.shape
    hid = cotangent.shape[1]
    groups = lax.axis_size(GRP)
    blocks = lax.axis_size(BLK)
    plane = lax.axis_size(PLANE)

    stale = lax.all_to_all(stale_part[0], GRP, 0, 0, tiled=True)
    same = lax.all_gather(node_feats, EVERY_OTHER)
    length = lax.axis_size(LINE)
    up = [(i, (i + 1) % length) for i in range(length)]
    down = [(i, (i - 1) % length) for i in range(length)]
    half = same.shape[0] // 2
    low, high = same[:half], same[half:]
    swap = [(0, 1), (1, 0)]
    side_low, side_high = lax.ppermute(low, "x_hi", swap), lax.ppermute(high, "x_hi", swap)
    banks = (
        low,
        high,
        lax.ppermute(low, LINE, up),
        lax.ppermute(high, LINE, down),
        side_low,
        side_high,
        lax.ppermute(side_low, LINE, up),
        lax.ppermute(side_high, LINE, down),
    )
    index = jnp.arange(blocks, dtype=jnp.int32)
    other_side = index // length != lax.axis_index("x_hi")
    other_parity = index % 2 != lax.axis_index("z_near")
    slot = index % length // 2
    place = slot + length // 2 * (other_parity.astype(jnp.int32) + 2 * other_side)
    own = lax.axis_index(GRP).reshape(1).astype(jnp.int32)

    smem = pl.BlockSpec(memory_space=pltpu.SMEM)
    vmem = pl.BlockSpec(memory_space=pltpu.VMEM)
    piece_rows = 2 * width // plane
    tile, slots = adj_tiles.shape[1], adj_tiles.shape[0]
    whole = pl.BlockSpec(memory_space=pl.ANY)
    bf16, f32 = jnp.bfloat16, jnp.float32
    limit = pltpu.CompilerParams(vmem_limit_bytes=32 * 1024 * 1024)
    stale_sum, base, w_neigh, cotangent = pl.pallas_call(
        early_kernel,
        out_shape=(
            jax.ShapeDtypeStruct((node_dev, width), f32),
            jax.ShapeDtypeStruct((node_dev, hid), f32),
            jax.ShapeDtypeStruct(w_neigh.shape, bf16),
            jax.ShapeDtypeStruct(cotangent.shape, bf16),
        ),
        in_specs=[smem] + [vmem] * 5,
        out_specs=(vmem,) * 4,
        compiler_params=limit,
        cost_estimate=pl.CostEstimate(
            flops=2 * node_dev * width * hid, bytes_accessed=2**20, transcendentals=0
        ),
    )(own, stale, node_feats, w_self, w_neigh, cotangent)
    hidden, grads, positions = pl.pallas_call(
        layer_kernel,
        out_shape=(
            jax.ShapeDtypeStruct((node_dev, hid), bf16),
            jax.ShapeDtypeStruct((plane, piece_rows, hid + hid // 2), bf16),
            jax.ShapeDtypeStruct(tile_pos.shape, jnp.int32),
        ),
        in_specs=[smem] * 4 + [whole, [whole] * len(banks)] + [vmem] * 6,
        out_specs=(vmem, vmem, smem),
        scratch_shapes=[
            pltpu.VMEM((slots, node_dev, tile), bf16),
            pltpu.VMEM((slots, tile, width), bf16),
            pltpu.SemaphoreType.DMA((slots,)),
            pltpu.SemaphoreType.DMA((slots, tile // node_dev)),
        ],
        compiler_params=limit,
        cost_estimate=pl.CostEstimate(
            flops=8 * node_dev * width * hid, bytes_accessed=2**20, transcendentals=0
        ),
    )(
        tile_count,
        tile_pos,
        place,
        own,
        adj_tiles,
        list(banks),
        stale_sum,
        base,
        node_feats,
        w_neigh,
        bias_vec[None],
        cotangent,
    )
    new_part = pl.pallas_call(
        partial_kernel,
        out_shape=jax.ShapeDtypeStruct((groups, node_dev, width), bf16),
        in_specs=[smem] * 3 + [vmem, [vmem] * len(banks)],
        out_specs=vmem,
        scratch_shapes=[
            pltpu.VMEM((groups * node_dev, width), f32),
            pltpu.VMEM((tile, width), bf16),
        ],
        compiler_params=limit,
        cost_estimate=pl.CostEstimate(
            flops=2 * slots * tile * tile * width, bytes_accessed=8 * 2**20, transcendentals=0
        ),
    )(tile_count, positions, place, adj_tiles, list(banks))

    scaling = float(node_dev * groups * blocks) ** (-0.5)
    piece = lax.all_to_all(grads, PLANE, 0, 0, tiled=True).astype(f32)
    piece = lax.all_gather(jnp.sum(piece, axis=0).astype(bf16), EVERY_OTHER).astype(f32)
    piece = jnp.sum(piece, axis=0)
    piece = (piece + lax.ppermute(piece, "z_near", swap)) * scaling
    grad_bias = piece[:2, hid:].reshape(hid)
    both = spread(piece[:, :hid].astype(bf16), PLANE).astype(f32).reshape(2 * width, hid)
    return new_part[None], hidden, both[:width], both[width:], grad_bias


def solution(mesh):
    fine = Mesh(mesh.devices.reshape(SIZES), ALL)
    placed = (
        P(ALL, None, None),
        P(ALL),
        P(ALL),
        P(ALL, None),
        P(GRP, None, BLK, None),
        P(),
        P(),
        P(),
        P(ALL, None),
    )
    return jax.shard_map(
        body,
        mesh=fine,
        in_specs=placed,
        out_specs=(P(GRP, None, BLK, None), P(ALL, None), P(), P(), P()),
        check_vma=False,
    )
```

```python
import jax
import jax.numpy as jnp
from jax import lax
from jax.experimental import pallas as pl
from jax.experimental.pallas import tpu as pltpu
from jax.sharding import Mesh, PartitionSpec as P

GRP = ("y", "x_lo", "core")
PLANE = ("y", "x_lo", "core", "x_hi")
LINE = ("z_far", "z_mid", "z_near")
EVERY_OTHER = ("z_far", "z_mid")
BLK = ("x_hi",) + LINE
ALL = GRP + BLK
SIZES = (4, 2, 2, 2, 8, 2, 2)


def spread(value, axes):
    copies = lax.axis_size(axes)
    return lax.all_to_all(
        jnp.broadcast_to(value[None], (copies,) + value.shape), axes, 0, 0, tiled=True
    )


def split_position(position, col_tiles, per_tile):
    return lax.div(position, col_tiles), lax.rem(position, col_tiles) * per_tile


def early_kernel(
    own_ref, stale_ref, feats_ref, w_self_ref, w_neigh_ref, cot_ref,
    sum_ref, base_ref, w_neigh_out, cot_out,
):
    groups = stale_ref.shape[0]
    own = own_ref[0]
    stale = jnp.zeros(sum_ref.shape, jnp.float32)
    for source in range(groups):
        keep = jnp.where(source == own, jnp.float32(0.0), jnp.float32(1.0))
        stale += stale_ref[source].astype(jnp.float32) * keep
    sum_ref[...] = stale
    preact = jnp.dot(feats_ref[...], w_self_ref[...], preferred_element_type=jnp.float32)
    base_ref[...] = preact
    w_neigh_out[...] = w_neigh_ref[...]
    cot_out[...] = cot_ref[...]


def layer_kernel(
    count_ref,
    pos_ref,
    place_ref,
    own_ref,
    adj_ref,
    bank_refs,
    stale_ref,
    base_ref,
    feats_ref,
    w_neigh_ref,
    bias_ref,
    cot_ref,
    hidden_ref,
    grads_ref,
    tiles_ref,
    sources_ref,
    tile_sem,
    source_sem,
):
    tile = adj_ref.shape[1]
    node_dev, width = stale_ref.shape
    per_tile = tile // node_dev
    bank_slots = 2 * bank_refs[0].shape[0]
    col_tiles = place_ref.shape[0] // per_tile
    own = own_ref[0]
    own_tile, own_part = lax.div(own, per_tile), lax.rem(own, per_tile)
    count = count_ref[0]

    def tile_copy(slot):
        rows = pl.ds(pl.multiple_of(own_part * node_dev, node_dev), node_dev)
        return pltpu.make_async_copy(
            adj_ref.at[slot, rows, :], tiles_ref.at[slot], tile_sem.at[slot]
        )

    def source_copy(slot, j, bank, block):
        return pltpu.make_async_copy(
            bank.at[block],
            sources_ref.at[slot, pl.ds(j * node_dev, node_dev), :],
            source_sem.at[slot, j],
        )

    def fetch(slot, carry):
        row_tile, first = split_position(pos_ref[slot], col_tiles, per_tile)

        @pl.when(row_tile == own_tile)
        def _():
            tile_copy(slot).start()
            for j in range(per_tile):
                place = place_ref[first + j]
                bank, block = lax.div(place, bank_slots), lax.rem(place, bank_slots)
                for choice, ref in enumerate(bank_refs):

                    @pl.when(bank == choice)
                    def _():
                        source_copy(slot, j, ref, block).start()

        return carry

    lax.fori_loop(0, count, fetch, 0)

    def add_tile(slot, fresh):
        row_tile, _ = split_position(pos_ref[slot], col_tiles, per_tile)

        def add():
            tile_copy(slot).wait()
            for j in range(per_tile):
                source_copy(slot, j, bank_refs[0], 0).wait()
            return fresh + jnp.dot(
                tiles_ref[slot], sources_ref[slot], preferred_element_type=jnp.float32
            )

        return lax.cond(row_tile == own_tile, add, lambda: fresh)

    fresh = lax.fori_loop(0, count, add_tile, jnp.zeros((node_dev, width), jnp.float32))
    aggregate = (fresh + stale_ref[...]).astype(jnp.bfloat16)
    feats = feats_ref[...]
    preact = base_ref[...]
    preact += jnp.dot(aggregate, w_neigh_ref[...], preferred_element_type=jnp.float32)
    preact += bias_ref[...]
    gate = jax.nn.sigmoid(preact)
    hidden_ref[...] = (preact * gate).astype(hidden_ref.dtype)
    grad_pre = (
        cot_ref[...].astype(jnp.float32) * gate * (1.0 + preact * (1.0 - gate))
    ).astype(jnp.bfloat16)
    both = jnp.concatenate([feats, aggregate], axis=1)
    grads = lax.dot_general(
        both, grad_pre, (((0,), (0,)), ((), ())), preferred_element_type=jnp.float32
    )
    bias_grad = jnp.sum(grad_pre.astype(jnp.float32), axis=0, keepdims=True)
    pieces, piece_rows, _ = grads_ref.shape
    hid = grads.shape[1]
    grads_ref[:, :, :hid] = grads.reshape(pieces, piece_rows, hid).astype(grads_ref.dtype)
    half = hid // 2
    tail = jnp.concatenate(
        [
            bias_grad[:, :half],
            bias_grad[:, half:],
            jnp.zeros((piece_rows - 2, half), jnp.float32),
        ],
        axis=0,
    )
    grads_ref[:, :, hid:] = jnp.broadcast_to(tail[None], (pieces, piece_rows, half)).astype(
        grads_ref.dtype
    )


def partial_kernel(
    count_ref, pos_ref, place_ref, adj_ref, bank_refs, _, part_ref, acc_ref, source_ref
):
    tile = adj_ref.shape[1]
    _, node_dev, _ = part_ref.shape
    per_tile = tile // node_dev
    bank_slots = 2 * bank_refs[0].shape[0]
    col_tiles = place_ref.shape[0] // per_tile
    acc_ref[...] = jnp.zeros_like(acc_ref)

    def add_tile(slot, carry):
        row_tile, first = split_position(pos_ref[slot], col_tiles, per_tile)
        for j in range(per_tile):
            place = place_ref[first + j]
            bank, block = lax.div(place, bank_slots), lax.rem(place, bank_slots)
            for choice, ref in enumerate(bank_refs):

                @pl.when(bank == choice)
                def _():
                    source_ref[j * node_dev : (j + 1) * node_dev, :] = ref[block]

        product = jnp.dot(adj_ref[slot], source_ref[...], preferred_element_type=jnp.float32)
        rows = pl.ds(pl.multiple_of(row_tile * tile, tile), tile)
        acc_ref[rows, :] += product
        return carry

    lax.fori_loop(0, count_ref[0], add_tile, 0)
    part_ref[...] = acc_ref[...].reshape(part_ref.shape).astype(part_ref.dtype)


def body(
    adj_tiles, tile_pos, tile_count, node_feats, stale_part, w_self, w_neigh, bias_vec, cotangent
):
    node_dev, width = node_feats.shape
    hid = cotangent.shape[1]
    groups = lax.axis_size(GRP)
    blocks = lax.axis_size(BLK)
    plane = lax.axis_size(PLANE)

    stale = lax.all_to_all(stale_part[0], GRP, 0, 0, tiled=True)
    same = lax.all_gather(node_feats, EVERY_OTHER)
    length = lax.axis_size(LINE)
    up = [(i, (i + 1) % length) for i in range(length)]
    down = [(i, (i - 1) % length) for i in range(length)]
    half = same.shape[0] // 2
    low, high = same[:half], same[half:]
    swap = [(0, 1), (1, 0)]
    side_low, side_high = lax.ppermute(low, "x_hi", swap), lax.ppermute(high, "x_hi", swap)
    beside = lax.ppermute(same, LINE, up)
    banks = (
        same,
        beside,
        side_low,
        side_high,
        lax.ppermute(side_low, LINE, down),
        lax.ppermute(side_high, LINE, up),
    )
    index = jnp.arange(blocks, dtype=jnp.int32)
    other_side = index // length != lax.axis_index("x_hi")
    other_parity = index % 2 != lax.axis_index("z_near")
    slot = index % length // 2
    low_bank = jnp.where(other_side, 2 + 2 * other_parity, other_parity)
    first = other_side & (slot >= half)
    place = (low_bank + first) * length + jnp.where(first, slot - half, slot)
    own = lax.axis_index(GRP).reshape(1).astype(jnp.int32)

    smem = pl.BlockSpec(memory_space=pltpu.SMEM)
    vmem = pl.BlockSpec(memory_space=pltpu.VMEM)
    piece_rows = 2 * width // plane
    tile, slots = adj_tiles.shape[1], adj_tiles.shape[0]
    whole = pl.BlockSpec(memory_space=pl.ANY)
    bf16, f32 = jnp.bfloat16, jnp.float32
    limit = pltpu.CompilerParams(vmem_limit_bytes=32 * 1024 * 1024)
    stale_sum, base, w_neigh, cotangent = pl.pallas_call(
        early_kernel,
        out_shape=(
            jax.ShapeDtypeStruct((node_dev, width), f32),
            jax.ShapeDtypeStruct((node_dev, hid), f32),
            jax.ShapeDtypeStruct(w_neigh.shape, bf16),
            jax.ShapeDtypeStruct(cotangent.shape, bf16),
        ),
        in_specs=[smem] + [vmem] * 5,
        out_specs=(vmem,) * 4,
        compiler_params=limit,
        cost_estimate=pl.CostEstimate(
            flops=2 * node_dev * width * hid, bytes_accessed=2**20, transcendentals=0
        ),
    )(own, stale, node_feats, w_self, w_neigh, cotangent)
    hidden, grads = pl.pallas_call(
        layer_kernel,
        out_shape=(
            jax.ShapeDtypeStruct((node_dev, hid), bf16),
            jax.ShapeDtypeStruct((plane, piece_rows, hid + hid // 2), bf16),
        ),
        in_specs=[smem] * 4 + [whole, [whole] * len(banks)] + [vmem] * 6,
        out_specs=(vmem, vmem),
        scratch_shapes=[
            pltpu.VMEM((slots, node_dev, tile), bf16),
            pltpu.VMEM((slots, tile, width), bf16),
            pltpu.SemaphoreType.DMA((slots,)),
            pltpu.SemaphoreType.DMA((slots, tile // node_dev)),
        ],
        compiler_params=limit,
        cost_estimate=pl.CostEstimate(
            flops=8 * node_dev * width * hid, bytes_accessed=2**20, transcendentals=0
        ),
    )(
        tile_count,
        tile_pos,
        place,
        own,
        adj_tiles,
        list(banks),
        stale_sum,
        base,
        node_feats,
        w_neigh,
        bias_vec[None],
        cotangent,
    )
    scaling = float(node_dev * groups * blocks) ** (-0.5)
    piece = lax.all_to_all(grads, PLANE, 0, 0, tiled=True).astype(f32)
    piece = lax.all_gather(jnp.sum(piece, axis=0).astype(bf16), EVERY_OTHER).astype(f32)
    piece = jnp.sum(piece, axis=0)
    piece = (piece + lax.ppermute(piece, "z_near", swap)) * scaling
    new_part = pl.pallas_call(
        partial_kernel,
        out_shape=jax.ShapeDtypeStruct((groups, node_dev, width), bf16),
        in_specs=[smem] * 3 + [vmem, [vmem] * len(banks), whole],
        out_specs=vmem,
        scratch_shapes=[
            pltpu.VMEM((groups * node_dev, width), f32),
            pltpu.VMEM((tile, width), bf16),
        ],
        compiler_params=limit,
        cost_estimate=pl.CostEstimate(
            flops=2 * slots * tile * tile * width, bytes_accessed=8 * 2**20, transcendentals=0
        ),
    )(tile_count, tile_pos, place, adj_tiles, list(banks), piece)
    grad_bias = piece[:2, hid:].reshape(hid)
    both = spread(piece[:, :hid].astype(bf16), PLANE).astype(f32).reshape(2 * width, hid)
    return new_part[None], hidden, both[:width], both[width:], grad_bias


def solution(mesh):
    fine = Mesh(mesh.devices.reshape(SIZES), ALL)
    placed = (
        P(ALL, None, None),
        P(ALL),
        P(ALL),
        P(ALL, None),
        P(GRP, None, BLK, None),
        P(),
        P(),
        P(),
        P(ALL, None),
    )
    return jax.shard_map(
        body,
        mesh=fine,
        in_specs=placed,
        out_specs=(P(GRP, None, BLK, None), P(ALL, None), P(), P(), P()),
        check_vma=False,
    )
```

```python
import jax
import jax.numpy as jnp
from jax import lax
from jax.experimental import pallas as pl
from jax.experimental.pallas import tpu as pltpu
from jax.sharding import Mesh, PartitionSpec as P

GRP = ("y", "x_lo", "core")
PLANE = ("y", "x_lo", "core", "x_hi")
LINE = ("z_far", "z_mid", "z_near")
EVERY_OTHER = ("z_far", "z_mid")
BLK = ("x_hi",) + LINE
ALL = GRP + BLK
SIZES = (4, 2, 2, 2, 8, 2, 2)


def spread(value, axes):
    copies = lax.axis_size(axes)
    return lax.all_to_all(
        jnp.broadcast_to(value[None], (copies,) + value.shape), axes, 0, 0, tiled=True
    )


def split_position(position, col_tiles, per_tile):
    return lax.div(position, col_tiles), lax.rem(position, col_tiles) * per_tile


def early_kernel(
    own_ref, stale_ref, feats_ref, w_self_ref, w_neigh_ref, cot_ref,
    sum_ref, base_ref, w_neigh_out, cot_out,
):
    groups = stale_ref.shape[0]
    own = own_ref[0]
    stale = jnp.zeros(sum_ref.shape, jnp.float32)
    for source in range(groups):
        keep = jnp.where(source == own, jnp.float32(0.0), jnp.float32(1.0))
        stale += stale_ref[source].astype(jnp.float32) * keep
    sum_ref[...] = stale
    preact = jnp.dot(feats_ref[...], w_self_ref[...], preferred_element_type=jnp.float32)
    base_ref[...] = preact
    w_neigh_out[...] = w_neigh_ref[...]
    cot_out[...] = cot_ref[...]


def layer_kernel(
    count_ref,
    pos_ref,
    place_ref,
    own_ref,
    adj_ref,
    bank_refs,
    stale_ref,
    base_ref,
    feats_ref,
    w_neigh_ref,
    bias_ref,
    cot_ref,
    hidden_ref,
    grads_ref,
    tiles_ref,
    sources_ref,
    tile_sem,
    source_sem,
):
    tile = adj_ref.shape[1]
    node_dev, width = stale_ref.shape
    per_tile = tile // node_dev
    bank_slots = 2 * bank_refs[0].shape[0]
    col_tiles = place_ref.shape[0] // per_tile
    own = own_ref[0]
    own_tile, own_part = lax.div(own, per_tile), lax.rem(own, per_tile)
    count = count_ref[0]

    def tile_copy(slot):
        rows = pl.ds(pl.multiple_of(own_part * node_dev, node_dev), node_dev)
        return pltpu.make_async_copy(
            adj_ref.at[slot, rows, :], tiles_ref.at[slot], tile_sem.at[slot]
        )

    def source_copy(slot, j, bank, block):
        return pltpu.make_async_copy(
            bank.at[block],
            sources_ref.at[slot, pl.ds(j * node_dev, node_dev), :],
            source_sem.at[slot, j],
        )

    def fetch(slot, carry):
        row_tile, first = split_position(pos_ref[slot], col_tiles, per_tile)

        @pl.when(row_tile == own_tile)
        def _():
            tile_copy(slot).start()
            for j in range(per_tile):
                place = place_ref[first + j]
                bank, block = lax.div(place, bank_slots), lax.rem(place, bank_slots)
                for choice, ref in enumerate(bank_refs):

                    @pl.when(bank == choice)
                    def _():
                        source_copy(slot, j, ref, block).start()

        return carry

    lax.fori_loop(0, count, fetch, 0)

    def add_tile(slot, fresh):
        row_tile, _ = split_position(pos_ref[slot], col_tiles, per_tile)

        def add():
            tile_copy(slot).wait()
            for j in range(per_tile):
                source_copy(slot, j, bank_refs[0], 0).wait()
            return fresh + jnp.dot(
                tiles_ref[slot], sources_ref[slot], preferred_element_type=jnp.float32
            )

        return lax.cond(row_tile == own_tile, add, lambda: fresh)

    fresh = lax.fori_loop(0, count, add_tile, jnp.zeros((node_dev, width), jnp.float32))
    aggregate = (fresh + stale_ref[...]).astype(jnp.bfloat16)
    feats = feats_ref[...]
    preact = base_ref[...]
    preact += jnp.dot(aggregate, w_neigh_ref[...], preferred_element_type=jnp.float32)
    preact += bias_ref[...]
    gate = jax.nn.sigmoid(preact)
    hidden_ref[...] = (preact * gate).astype(hidden_ref.dtype)
    grad_pre = (
        cot_ref[...].astype(jnp.float32) * gate * (1.0 + preact * (1.0 - gate))
    ).astype(jnp.bfloat16)
    both = jnp.concatenate([feats, aggregate], axis=1)
    grads = lax.dot_general(
        both, grad_pre, (((0,), (0,)), ((), ())), preferred_element_type=jnp.float32
    )
    bias_grad = jnp.sum(grad_pre.astype(jnp.float32), axis=0, keepdims=True)
    pieces, piece_rows, _ = grads_ref.shape
    hid = grads.shape[1]
    grads_ref[:, :, :hid] = grads.reshape(pieces, piece_rows, hid).astype(grads_ref.dtype)
    half = hid // 2
    tail = jnp.concatenate(
        [
            bias_grad[:, :half],
            bias_grad[:, half:],
            jnp.zeros((piece_rows - 2, half), jnp.float32),
        ],
        axis=0,
    )
    grads_ref[:, :, hid:] = jnp.broadcast_to(tail[None], (pieces, piece_rows, half)).astype(
        grads_ref.dtype
    )


def partial_kernel(
    count_ref,
    pos_ref,
    place_ref,
    adj_ref,
    bank_refs,
    _,
    part_ref,
    acc_ref,
    source_ref,
    tiles_ref,
    tile_sem,
):
    tile = adj_ref.shape[1]
    _, node_dev, _ = part_ref.shape
    per_tile = tile // node_dev
    bank_slots = 2 * bank_refs[0].shape[0]
    col_tiles = place_ref.shape[0] // per_tile
    count = count_ref[0]

    def tile_copy(slot):
        return pltpu.make_async_copy(adj_ref.at[slot], tiles_ref.at[slot], tile_sem.at[slot])

    def fetch(slot, carry):
        tile_copy(slot).start()
        return carry

    lax.fori_loop(0, count, fetch, 0)
    acc_ref[...] = jnp.zeros_like(acc_ref)

    def add_tile(slot, carry):
        row_tile, first = split_position(pos_ref[slot], col_tiles, per_tile)
        for j in range(per_tile):
            place = place_ref[first + j]
            bank, block = lax.div(place, bank_slots), lax.rem(place, bank_slots)
            for choice, ref in enumerate(bank_refs):

                @pl.when(bank == choice)
                def _():
                    source_ref[j * node_dev : (j + 1) * node_dev, :] = ref[block]

        tile_copy(slot).wait()
        product = jnp.dot(tiles_ref[slot], source_ref[...], preferred_element_type=jnp.float32)
        rows = pl.ds(pl.multiple_of(row_tile * tile, tile), tile)
        acc_ref[rows, :] += product
        return carry

    lax.fori_loop(0, count, add_tile, 0)
    part_ref[...] = acc_ref[...].reshape(part_ref.shape).astype(part_ref.dtype)


def body(
    adj_tiles, tile_pos, tile_count, node_feats, stale_part, w_self, w_neigh, bias_vec, cotangent
):
    node_dev, width = node_feats.shape
    hid = cotangent.shape[1]
    groups = lax.axis_size(GRP)
    blocks = lax.axis_size(BLK)
    plane = lax.axis_size(PLANE)

    stale = lax.all_to_all(stale_part[0], GRP, 0, 0, tiled=True)
    same = lax.all_gather(node_feats, EVERY_OTHER)
    length = lax.axis_size(LINE)
    up = [(i, (i + 1) % length) for i in range(length)]
    down = [(i, (i - 1) % length) for i in range(length)]
    cut = same.shape[0] // 2
    low, high = same[:cut], same[cut:]
    swap = [(0, 1), (1, 0)]
    side_low, side_high = lax.ppermute(low, "x_hi", swap), lax.ppermute(high, "x_hi", swap)
    beside = lax.ppermute(same, LINE, up)
    banks = (
        same,
        beside,
        side_low,
        side_high,
        lax.ppermute(side_low, LINE, down),
        lax.ppermute(side_high, LINE, up),
    )
    index = jnp.arange(blocks, dtype=jnp.int32)
    other_side = index // length != lax.axis_index("x_hi")
    other_parity = index % 2 != lax.axis_index("z_near")
    slot = index % length // 2
    low_bank = jnp.where(other_side, 2 + 2 * other_parity, other_parity)
    first = other_side & (slot >= cut)
    place = (low_bank + first) * length + jnp.where(first, slot - cut, slot)
    own = lax.axis_index(GRP).reshape(1).astype(jnp.int32)

    smem = pl.BlockSpec(memory_space=pltpu.SMEM)
    vmem = pl.BlockSpec(memory_space=pltpu.VMEM)
    piece_rows = 2 * width // plane
    tile, slots = adj_tiles.shape[1], adj_tiles.shape[0]
    whole = pl.BlockSpec(memory_space=pl.ANY)
    hbm = pl.BlockSpec(memory_space=pltpu.HBM)
    bf16, f32 = jnp.bfloat16, jnp.float32
    limit = pltpu.CompilerParams(vmem_limit_bytes=32 * 1024 * 1024)
    most = pltpu.CompilerParams(vmem_limit_bytes=62 * 1024 * 1024)
    stale_sum, base, w_neigh, cotangent = pl.pallas_call(
        early_kernel,
        out_shape=(
            jax.ShapeDtypeStruct((node_dev, width), f32),
            jax.ShapeDtypeStruct((node_dev, hid), f32),
            jax.ShapeDtypeStruct(w_neigh.shape, bf16),
            jax.ShapeDtypeStruct(cotangent.shape, bf16),
        ),
        in_specs=[smem] + [vmem] * 5,
        out_specs=(vmem,) * 4,
        compiler_params=limit,
        cost_estimate=pl.CostEstimate(
            flops=2 * node_dev * width * hid, bytes_accessed=2**20, transcendentals=0
        ),
    )(own, stale, node_feats, w_self, w_neigh, cotangent)
    hidden, grads = pl.pallas_call(
        layer_kernel,
        out_shape=(
            jax.ShapeDtypeStruct((node_dev, hid), bf16),
            jax.ShapeDtypeStruct((plane, piece_rows, hid + hid // 2), bf16),
        ),
        in_specs=[smem] * 4 + [hbm, [whole] * len(banks)] + [vmem] * 6,
        out_specs=(vmem, vmem),
        scratch_shapes=[
            pltpu.VMEM((slots, node_dev, tile), bf16),
            pltpu.VMEM((slots, tile, width), bf16),
            pltpu.SemaphoreType.DMA((slots,)),
            pltpu.SemaphoreType.DMA((slots, tile // node_dev)),
        ],
        compiler_params=limit,
        cost_estimate=pl.CostEstimate(
            flops=8 * node_dev * width * hid, bytes_accessed=2**20, transcendentals=0
        ),
    )(
        tile_count,
        tile_pos,
        place,
        own,
        adj_tiles,
        list(banks),
        stale_sum,
        base,
        node_feats,
        w_neigh,
        bias_vec[None],
        cotangent,
    )
    scaling = float(node_dev * groups * blocks) ** (-0.5)
    piece = lax.all_to_all(grads, PLANE, 0, 0, tiled=True).astype(f32)
    piece = lax.all_gather(jnp.sum(piece, axis=0).astype(bf16), EVERY_OTHER).astype(f32)
    piece = jnp.sum(piece, axis=0)
    piece = (piece + lax.ppermute(piece, "z_near", swap)) * scaling
    new_part = pl.pallas_call(
        partial_kernel,
        out_shape=jax.ShapeDtypeStruct((groups, node_dev, width), bf16),
        in_specs=[smem] * 3 + [hbm, [vmem] * len(banks), whole],
        out_specs=vmem,
        scratch_shapes=[
            pltpu.VMEM((groups * node_dev, width), f32),
            pltpu.VMEM((tile, width), bf16),
            pltpu.VMEM((slots, tile, tile), bf16),
            pltpu.SemaphoreType.DMA((slots,)),
        ],
        compiler_params=most,
        cost_estimate=pl.CostEstimate(
            flops=2 * slots * tile * tile * width, bytes_accessed=8 * 2**20, transcendentals=0
        ),
    )(tile_count, tile_pos, place, adj_tiles, list(banks), piece)
    grad_bias = piece[:2, hid:].reshape(hid)
    both = spread(piece[:, :hid].astype(bf16), PLANE).astype(f32).reshape(2 * width, hid)
    return new_part[None], hidden, both[:width], both[width:], grad_bias


def solution(mesh):
    fine = Mesh(mesh.devices.reshape(SIZES), ALL)
    placed = (
        P(ALL, None, None),
        P(ALL),
        P(ALL),
        P(ALL, None),
        P(GRP, None, BLK, None),
        P(),
        P(),
        P(),
        P(ALL, None),
    )
    return jax.shard_map(
        body,
        mesh=fine,
        in_specs=placed,
        out_specs=(P(GRP, None, BLK, None), P(ALL, None), P(), P(), P()),
        check_vma=False,
    )
```

```python
import jax
import jax.numpy as jnp
from jax import lax
from jax.experimental import pallas as pl
from jax.experimental.pallas import tpu as pltpu
from jax.sharding import Mesh, PartitionSpec as P

GRP = ("y", "x_lo", "core")
PLANE = ("y", "x_lo", "core", "x_hi")
LINE = ("z_far", "z_mid", "z_near")
EVERY_OTHER = ("z_far", "z_mid")
BLK = ("x_hi",) + LINE
ALL = GRP + BLK
SIZES = (4, 2, 2, 2, 8, 2, 2)


def split_position(position, col_tiles, per_tile):
    return lax.div(position, col_tiles), lax.rem(position, col_tiles) * per_tile


def early_kernel(
    own_ref, stale_ref, feats_ref, w_self_ref, w_neigh_ref, cot_ref,
    sum_ref, base_ref, w_neigh_out, cot_out,
):
    groups = stale_ref.shape[0]
    own = own_ref[0]
    stale = jnp.zeros(sum_ref.shape, jnp.float32)
    for source in range(groups):
        keep = jnp.where(source == own, jnp.float32(0.0), jnp.float32(1.0))
        stale += stale_ref[source].astype(jnp.float32) * keep
    sum_ref[...] = stale
    preact = jnp.dot(feats_ref[...], w_self_ref[...], preferred_element_type=jnp.float32)
    base_ref[...] = preact
    w_neigh_out[...] = w_neigh_ref[...]
    cot_out[...] = cot_ref[...]


def layer_kernel(
    count_ref,
    pos_ref,
    place_ref,
    own_ref,
    adj_ref,
    bank_refs,
    stale_ref,
    base_ref,
    feats_ref,
    w_neigh_ref,
    bias_ref,
    cot_ref,
    hidden_ref,
    grads_ref,
    tiles_ref,
    sources_ref,
    tile_sem,
    source_sem,
):
    tile = adj_ref.shape[1]
    node_dev, width = stale_ref.shape
    per_tile = tile // node_dev
    bank_slots = 2 * bank_refs[0].shape[0]
    col_tiles = place_ref.shape[0] // per_tile
    own = own_ref[0]
    own_tile, own_part = lax.div(own, per_tile), lax.rem(own, per_tile)
    count = count_ref[0]

    def tile_copy(slot):
        rows = pl.ds(pl.multiple_of(own_part * node_dev, node_dev), node_dev)
        return pltpu.make_async_copy(
            adj_ref.at[slot, rows, :], tiles_ref.at[slot], tile_sem.at[slot]
        )

    def source_copy(slot, j, bank, block):
        return pltpu.make_async_copy(
            bank.at[block],
            sources_ref.at[slot, pl.ds(j * node_dev, node_dev), :],
            source_sem.at[slot, j],
        )

    def fetch(slot, carry):
        row_tile, first = split_position(pos_ref[slot], col_tiles, per_tile)

        @pl.when(row_tile == own_tile)
        def _():
            tile_copy(slot).start()
            for j in range(per_tile):
                place = place_ref[first + j]
                bank, block = lax.div(place, bank_slots), lax.rem(place, bank_slots)
                for choice, ref in enumerate(bank_refs):

                    @pl.when(bank == choice)
                    def _():
                        source_copy(slot, j, ref, block).start()

        return carry

    lax.fori_loop(0, count, fetch, 0)

    def add_tile(slot, fresh):
        row_tile, _ = split_position(pos_ref[slot], col_tiles, per_tile)

        def add():
            tile_copy(slot).wait()
            for j in range(per_tile):
                source_copy(slot, j, bank_refs[0], 0).wait()
            return fresh + jnp.dot(
                tiles_ref[slot], sources_ref[slot], preferred_element_type=jnp.float32
            )

        return lax.cond(row_tile == own_tile, add, lambda: fresh)

    fresh = lax.fori_loop(0, count, add_tile, jnp.zeros((node_dev, width), jnp.float32))
    aggregate = (fresh + stale_ref[...]).astype(jnp.bfloat16)
    feats = feats_ref[...]
    preact = base_ref[...]
    preact += jnp.dot(aggregate, w_neigh_ref[...], preferred_element_type=jnp.float32)
    preact += bias_ref[...]
    gate = jax.nn.sigmoid(preact)
    hidden_ref[...] = (preact * gate).astype(hidden_ref.dtype)
    grad_pre = (
        cot_ref[...].astype(jnp.float32) * gate * (1.0 + preact * (1.0 - gate))
    ).astype(jnp.bfloat16)
    both = jnp.concatenate([feats, aggregate], axis=1)
    grads = lax.dot_general(
        both, grad_pre, (((0,), (0,)), ((), ())), preferred_element_type=jnp.float32
    )
    bias_grad = jnp.sum(grad_pre.astype(jnp.float32), axis=0, keepdims=True)
    pieces, piece_rows, _ = grads_ref.shape
    hid = grads.shape[1]
    grads_ref[:, :, :hid] = grads.reshape(pieces, piece_rows, hid).astype(grads_ref.dtype)
    half = hid // 2
    tail = jnp.concatenate(
        [
            bias_grad[:, :half],
            bias_grad[:, half:],
            jnp.zeros((piece_rows - 2, half), jnp.float32),
        ],
        axis=0,
    )
    grads_ref[:, :, hid:] = jnp.broadcast_to(tail[None], (pieces, piece_rows, half)).astype(
        grads_ref.dtype
    )


def partial_kernel(
    count_ref,
    pos_ref,
    place_ref,
    adj_ref,
    bank_refs,
    _,
    part_ref,
    acc_ref,
    source_ref,
    tiles_ref,
    tile_sem,
):
    tile = adj_ref.shape[1]
    _, node_dev, _ = part_ref.shape
    per_tile = tile // node_dev
    bank_slots = 2 * bank_refs[0].shape[0]
    col_tiles = place_ref.shape[0] // per_tile
    count = count_ref[0]

    def tile_copy(slot):
        return pltpu.make_async_copy(adj_ref.at[slot], tiles_ref.at[slot], tile_sem.at[slot])

    def fetch(slot, carry):
        tile_copy(slot).start()
        return carry

    lax.fori_loop(0, count, fetch, 0)
    acc_ref[...] = jnp.zeros_like(acc_ref)

    def add_tile(slot, carry):
        row_tile, first = split_position(pos_ref[slot], col_tiles, per_tile)
        for j in range(per_tile):
            place = place_ref[first + j]
            bank, block = lax.div(place, bank_slots), lax.rem(place, bank_slots)
            for choice, ref in enumerate(bank_refs):

                @pl.when(bank == choice)
                def _():
                    source_ref[j * node_dev : (j + 1) * node_dev, :] = ref[block]

        tile_copy(slot).wait()
        product = jnp.dot(tiles_ref[slot], source_ref[...], preferred_element_type=jnp.float32)
        rows = pl.ds(pl.multiple_of(row_tile * tile, tile), tile)
        acc_ref[rows, :] += product
        return carry

    lax.fori_loop(0, count, add_tile, 0)
    part_ref[...] = acc_ref[...].reshape(part_ref.shape).astype(part_ref.dtype)


def body(
    adj_tiles, tile_pos, tile_count, node_feats, stale_part, w_self, w_neigh, bias_vec, cotangent
):
    node_dev, width = node_feats.shape
    hid = cotangent.shape[1]
    groups = lax.axis_size(GRP)
    blocks = lax.axis_size(BLK)
    plane = lax.axis_size(PLANE)

    stale = lax.all_to_all(stale_part[0], GRP, 0, 0, tiled=True)
    same = lax.all_gather(node_feats, EVERY_OTHER)
    length = lax.axis_size(LINE)
    up = [(i, (i + 1) % length) for i in range(length)]
    down = [(i, (i - 1) % length) for i in range(length)]
    cut = same.shape[0] // 2
    low, high = same[:cut], same[cut:]
    swap = [(0, 1), (1, 0)]
    side_low, side_high = lax.ppermute(low, "x_hi", swap), lax.ppermute(high, "x_hi", swap)
    beside = lax.ppermute(same, LINE, up)
    banks = (
        same,
        beside,
        side_low,
        side_high,
        lax.ppermute(side_low, LINE, down),
        lax.ppermute(side_high, LINE, up),
    )
    index = jnp.arange(blocks, dtype=jnp.int32)
    other_side = index // length != lax.axis_index("x_hi")
    other_parity = index % 2 != lax.axis_index("z_near")
    slot = index % length // 2
    low_bank = jnp.where(other_side, 2 + 2 * other_parity, other_parity)
    first = other_side & (slot >= cut)
    place = (low_bank + first) * length + jnp.where(first, slot - cut, slot)
    own = lax.axis_index(GRP).reshape(1).astype(jnp.int32)

    smem = pl.BlockSpec(memory_space=pltpu.SMEM)
    vmem = pl.BlockSpec(memory_space=pltpu.VMEM)
    piece_rows = 2 * width // plane
    tile, slots = adj_tiles.shape[1], adj_tiles.shape[0]
    whole = pl.BlockSpec(memory_space=pl.ANY)
    hbm = pl.BlockSpec(memory_space=pltpu.HBM)
    bf16, f32 = jnp.bfloat16, jnp.float32
    limit = pltpu.CompilerParams(vmem_limit_bytes=32 * 1024 * 1024)
    broad = pltpu.CompilerParams(vmem_limit_bytes=51 * 1024 * 1024)
    most = pltpu.CompilerParams(vmem_limit_bytes=62 * 1024 * 1024)
    stale_sum, base, w_neigh, cotangent = pl.pallas_call(
        early_kernel,
        out_shape=(
            jax.ShapeDtypeStruct((node_dev, width), f32),
            jax.ShapeDtypeStruct((node_dev, hid), f32),
            jax.ShapeDtypeStruct(w_neigh.shape, bf16),
            jax.ShapeDtypeStruct(cotangent.shape, bf16),
        ),
        in_specs=[smem] + [vmem] * 5,
        out_specs=(vmem,) * 4,
        compiler_params=limit,
        cost_estimate=pl.CostEstimate(
            flops=2 * node_dev * width * hid, bytes_accessed=2**20, transcendentals=0
        ),
    )(own, stale, node_feats, w_self, w_neigh, cotangent)
    hidden, grads = pl.pallas_call(
        layer_kernel,
        out_shape=(
            jax.ShapeDtypeStruct((node_dev, hid), bf16),
            jax.ShapeDtypeStruct((plane, piece_rows, hid + hid // 2), bf16),
        ),
        in_specs=[smem] * 4 + [hbm, [whole] * len(banks)] + [vmem] * 6,
        out_specs=(vmem, vmem),
        scratch_shapes=[
            pltpu.VMEM((slots, node_dev, tile), bf16),
            pltpu.VMEM((slots, tile, width), bf16),
            pltpu.SemaphoreType.DMA((slots,)),
            pltpu.SemaphoreType.DMA((slots, tile // node_dev)),
        ],
        compiler_params=broad,
        cost_estimate=pl.CostEstimate(
            flops=8 * node_dev * width * hid, bytes_accessed=2**20, transcendentals=0
        ),
    )(
        tile_count,
        tile_pos,
        place,
        own,
        adj_tiles,
        list(banks),
        stale_sum,
        base,
        node_feats,
        w_neigh,
        bias_vec[None],
        cotangent,
    )
    scaling = float(node_dev * groups * blocks) ** (-0.5)
    piece = lax.all_to_all(grads, PLANE, 0, 0, tiled=True).astype(f32)
    piece = lax.all_gather(jnp.sum(piece, axis=0).astype(bf16), EVERY_OTHER).astype(f32)
    piece = jnp.sum(piece, axis=0)
    piece = (piece + lax.ppermute(piece, "z_near", swap)) * scaling
    grad_bias = piece[:2, hid:].reshape(hid)
    copies = jnp.broadcast_to(piece[None, :, :hid].astype(bf16), (plane, piece_rows, hid))
    both = lax.all_to_all(copies, PLANE, 0, 0, tiled=True).astype(f32).reshape(2 * width, hid)
    new_part = pl.pallas_call(
        partial_kernel,
        out_shape=jax.ShapeDtypeStruct((groups, node_dev, width), bf16),
        in_specs=[smem] * 3 + [hbm, [vmem] * len(banks), whole],
        out_specs=vmem,
        scratch_shapes=[
            pltpu.VMEM((groups * node_dev, width), f32),
            pltpu.VMEM((tile, width), bf16),
            pltpu.VMEM((slots, tile, tile), bf16),
            pltpu.SemaphoreType.DMA((slots,)),
        ],
        compiler_params=most,
        cost_estimate=pl.CostEstimate(
            flops=2 * slots * tile * tile * width, bytes_accessed=8 * 2**20, transcendentals=0
        ),
    )(tile_count, tile_pos, place, adj_tiles, list(banks), copies)
    return new_part[None], hidden, both[:width], both[width:], grad_bias


def solution(mesh):
    fine = Mesh(mesh.devices.reshape(SIZES), ALL)
    placed = (
        P(ALL, None, None),
        P(ALL),
        P(ALL),
        P(ALL, None),
        P(GRP, None, BLK, None),
        P(),
        P(),
        P(),
        P(ALL, None),
    )
    return jax.shard_map(
        body,
        mesh=fine,
        in_specs=placed,
        out_specs=(P(GRP, None, BLK, None), P(ALL, None), P(), P(), P()),
        check_vma=False,
    )
```

```python
import jax
import jax.numpy as jnp
from jax import lax
from jax.experimental import pallas as pl
from jax.experimental.pallas import tpu as pltpu
from jax.sharding import Mesh, PartitionSpec as P

GRP = ("y", "x_lo", "core")
PLANE = ("y", "x_lo", "core", "x_hi")
LINE = ("z_far", "z_mid", "z_near")
EVERY_OTHER = ("z_far", "z_mid")
BLK = ("x_hi",) + LINE
ALL = GRP + BLK
SIZES = (4, 2, 2, 2, 8, 2, 2)


def split_position(position, col_tiles, per_tile):
    return lax.div(position, col_tiles), lax.rem(position, col_tiles) * per_tile


def early_kernel(
    own_ref, stale_ref, feats_ref, w_self_ref, w_neigh_ref, cot_ref,
    sum_ref, base_ref, w_neigh_out, cot_out,
):
    groups = stale_ref.shape[0]
    own = own_ref[0]
    stale = jnp.zeros(sum_ref.shape, jnp.float32)
    for source in range(groups):
        keep = jnp.where(source == own, jnp.float32(0.0), jnp.float32(1.0))
        stale += stale_ref[source].astype(jnp.float32) * keep
    sum_ref[...] = stale
    preact = jnp.dot(feats_ref[...], w_self_ref[...], preferred_element_type=jnp.float32)
    base_ref[...] = preact
    w_neigh_out[...] = w_neigh_ref[...]
    cot_out[...] = cot_ref[...]


def layer_kernel(
    count_ref,
    pos_ref,
    place_ref,
    own_ref,
    adj_ref,
    bank_refs,
    stale_ref,
    base_ref,
    feats_ref,
    w_neigh_ref,
    bias_ref,
    cot_ref,
    hidden_ref,
    grads_ref,
    tiles_ref,
    sources_ref,
    tile_sem,
    source_sem,
):
    tile = adj_ref.shape[1]
    node_dev, width = stale_ref.shape
    per_tile = tile // node_dev
    bank_slots = 2 * bank_refs[0].shape[0]
    col_tiles = place_ref.shape[0] // per_tile
    own = own_ref[0]
    own_tile, own_part = lax.div(own, per_tile), lax.rem(own, per_tile)
    count = count_ref[0]

    def tile_copy(slot):
        rows = pl.ds(pl.multiple_of(own_part * node_dev, node_dev), node_dev)
        return pltpu.make_async_copy(
            adj_ref.at[slot, rows, :], tiles_ref.at[slot], tile_sem.at[slot]
        )

    def source_copy(slot, j, bank, block):
        return pltpu.make_async_copy(
            bank.at[block],
            sources_ref.at[slot, pl.ds(j * node_dev, node_dev), :],
            source_sem.at[slot, j],
        )

    def fetch(slot, carry):
        row_tile, first = split_position(pos_ref[slot], col_tiles, per_tile)

        @pl.when(row_tile == own_tile)
        def _():
            tile_copy(slot).start()
            for j in range(per_tile):
                place = place_ref[first + j]
                bank, block = lax.div(place, bank_slots), lax.rem(place, bank_slots)
                for choice, ref in enumerate(bank_refs):

                    @pl.when(bank == choice)
                    def _():
                        source_copy(slot, j, ref, block).start()

        return carry

    lax.fori_loop(0, count, fetch, 0)

    def add_tile(slot, fresh):
        row_tile, _ = split_position(pos_ref[slot], col_tiles, per_tile)

        def add():
            tile_copy(slot).wait()
            for j in range(per_tile):
                source_copy(slot, j, bank_refs[0], 0).wait()
            return fresh + jnp.dot(
                tiles_ref[slot], sources_ref[slot], preferred_element_type=jnp.float32
            )

        return lax.cond(row_tile == own_tile, add, lambda: fresh)

    fresh = lax.fori_loop(0, count, add_tile, jnp.zeros((node_dev, width), jnp.float32))
    aggregate = (fresh + stale_ref[...]).astype(jnp.bfloat16)
    feats = feats_ref[...]
    preact = base_ref[...]
    preact += jnp.dot(aggregate, w_neigh_ref[...], preferred_element_type=jnp.float32)
    preact += bias_ref[...]
    gate = jax.nn.sigmoid(preact)
    hidden_ref[...] = (preact * gate).astype(hidden_ref.dtype)
    grad_pre = (
        cot_ref[...].astype(jnp.float32) * gate * (1.0 + preact * (1.0 - gate))
    ).astype(jnp.bfloat16)
    both = jnp.concatenate([feats, aggregate], axis=1)
    grads = lax.dot_general(
        both, grad_pre, (((0,), (0,)), ((), ())), preferred_element_type=jnp.float32
    )
    bias_grad = jnp.sum(grad_pre.astype(jnp.float32), axis=0, keepdims=True)
    pieces, piece_rows, _ = grads_ref.shape
    hid = grads.shape[1]
    grads_ref[:, :, :hid] = grads.reshape(pieces, piece_rows, hid).astype(grads_ref.dtype)
    half = hid // 2
    tail = jnp.concatenate(
        [
            bias_grad[:, :half],
            bias_grad[:, half:],
            jnp.zeros((piece_rows - 2, half), jnp.float32),
        ],
        axis=0,
    )
    grads_ref[:, :, hid:] = jnp.broadcast_to(tail[None], (pieces, piece_rows, half)).astype(
        grads_ref.dtype
    )


def partial_kernel(
    count_ref,
    pos_ref,
    place_ref,
    adj_ref,
    bank_refs,
    _,
    part_ref,
    acc_ref,
    source_ref,
    tiles_ref,
    tile_sem,
):
    tile = adj_ref.shape[1]
    _, node_dev, _ = part_ref.shape
    per_tile = tile // node_dev
    bank_slots = 2 * bank_refs[0].shape[0]
    col_tiles = place_ref.shape[0] // per_tile
    count = count_ref[0]

    def tile_copy(slot):
        return pltpu.make_async_copy(adj_ref.at[slot], tiles_ref.at[slot], tile_sem.at[slot])

    def fetch(slot, carry):
        tile_copy(slot).start()
        return carry

    lax.fori_loop(0, count, fetch, 0)
    acc_ref[...] = jnp.zeros_like(acc_ref)

    def add_tile(slot, carry):
        row_tile, first = split_position(pos_ref[slot], col_tiles, per_tile)
        for j in range(per_tile):
            place = place_ref[first + j]
            bank, block = lax.div(place, bank_slots), lax.rem(place, bank_slots)
            for choice, ref in enumerate(bank_refs):

                @pl.when(bank == choice)
                def _():
                    source_ref[j * node_dev : (j + 1) * node_dev, :] = ref[block]

        tile_copy(slot).wait()
        product = jnp.dot(tiles_ref[slot], source_ref[...], preferred_element_type=jnp.float32)
        rows = pl.ds(pl.multiple_of(row_tile * tile, tile), tile)
        acc_ref[rows, :] += product
        return carry

    lax.fori_loop(0, count, add_tile, 0)
    part_ref[...] = acc_ref[...].reshape(part_ref.shape).astype(part_ref.dtype)


def body(
    adj_tiles, tile_pos, tile_count, node_feats, stale_part, w_self, w_neigh, bias_vec, cotangent
):
    node_dev, width = node_feats.shape
    hid = cotangent.shape[1]
    groups = lax.axis_size(GRP)
    blocks = lax.axis_size(BLK)
    plane = lax.axis_size(PLANE)

    stale = lax.all_to_all(stale_part[0], GRP, 0, 0, tiled=True)
    same = lax.all_gather(node_feats, EVERY_OTHER)
    length = lax.axis_size(LINE)
    up = [(i, (i + 1) % length) for i in range(length)]
    down = [(i, (i - 1) % length) for i in range(length)]
    cut = same.shape[0] // 2
    low, high = same[:cut], same[cut:]
    swap = [(0, 1), (1, 0)]
    side_low, side_high = lax.ppermute(low, "x_hi", swap), lax.ppermute(high, "x_hi", swap)
    beside = lax.ppermute(same, LINE, up)
    banks = (
        same,
        beside,
        side_low,
        side_high,
        lax.ppermute(side_low, LINE, down),
        lax.ppermute(side_high, LINE, up),
    )
    index = jnp.arange(blocks, dtype=jnp.int32)
    other_side = index // length != lax.axis_index("x_hi")
    other_parity = index % 2 != lax.axis_index("z_near")
    slot = index % length // 2
    low_bank = jnp.where(other_side, 2 + 2 * other_parity, other_parity)
    first = other_side & (slot >= cut)
    place = (low_bank + first) * length + jnp.where(first, slot - cut, slot)
    own = lax.axis_index(GRP).reshape(1).astype(jnp.int32)

    smem = pl.BlockSpec(memory_space=pltpu.SMEM)
    vmem = pl.BlockSpec(memory_space=pltpu.VMEM)
    piece_rows = 2 * width // plane
    tile, slots = adj_tiles.shape[1], adj_tiles.shape[0]
    whole = pl.BlockSpec(memory_space=pl.ANY)
    hbm = pl.BlockSpec(memory_space=pltpu.HBM)
    bf16, f32 = jnp.bfloat16, jnp.float32
    limit = pltpu.CompilerParams(vmem_limit_bytes=32 * 1024 * 1024)
    broad = pltpu.CompilerParams(vmem_limit_bytes=51 * 1024 * 1024)
    most = pltpu.CompilerParams(vmem_limit_bytes=62 * 1024 * 1024)
    stale_sum, base, w_neigh, cotangent = pl.pallas_call(
        early_kernel,
        out_shape=(
            jax.ShapeDtypeStruct((node_dev, width), f32),
            jax.ShapeDtypeStruct((node_dev, hid), f32),
            jax.ShapeDtypeStruct(w_neigh.shape, bf16),
            jax.ShapeDtypeStruct(cotangent.shape, bf16),
        ),
        in_specs=[smem] + [vmem] * 5,
        out_specs=(vmem,) * 4,
        compiler_params=limit,
        cost_estimate=pl.CostEstimate(
            flops=2 * node_dev * width * hid, bytes_accessed=2**20, transcendentals=0
        ),
    )(own, stale, node_feats, w_self, w_neigh, cotangent)
    hidden, grads = pl.pallas_call(
        layer_kernel,
        out_shape=(
            jax.ShapeDtypeStruct((node_dev, hid), bf16),
            jax.ShapeDtypeStruct((plane, piece_rows, hid + hid // 2), bf16),
        ),
        in_specs=[smem] * 4 + [hbm, [whole] * len(banks)] + [vmem] * 6,
        out_specs=(vmem, vmem),
        scratch_shapes=[
            pltpu.VMEM((slots, node_dev, tile), bf16),
            pltpu.VMEM((slots, tile, width), bf16),
            pltpu.SemaphoreType.DMA((slots,)),
            pltpu.SemaphoreType.DMA((slots, tile // node_dev)),
        ],
        compiler_params=broad,
        cost_estimate=pl.CostEstimate(
            flops=8 * node_dev * width * hid, bytes_accessed=2**20, transcendentals=0
        ),
    )(
        tile_count,
        tile_pos,
        place,
        own,
        adj_tiles,
        list(banks),
        stale_sum,
        base,
        node_feats,
        w_neigh,
        bias_vec[None],
        cotangent,
    )
    scaling = float(node_dev * groups * blocks) ** (-0.5)
    piece = lax.all_to_all(grads, PLANE, 0, 0, tiled=True).astype(f32)
    piece = lax.all_gather(jnp.sum(piece, axis=0).astype(bf16), EVERY_OTHER).astype(f32)
    piece = (jnp.sum(piece, axis=0) * scaling).astype(bf16)
    pair = plane * lax.axis_size("z_near")
    copies = jnp.broadcast_to(piece[None], (pair,) + piece.shape)
    both = lax.all_to_all(copies, PLANE + ("z_near",), 0, 0, tiled=True).astype(f32)
    both = jnp.sum(both.reshape((plane, 2) + piece.shape), axis=1)
    grad_bias = both[0, :2, hid:].reshape(hid)
    both = both[:, :, :hid].reshape(2 * width, hid)
    new_part = pl.pallas_call(
        partial_kernel,
        out_shape=jax.ShapeDtypeStruct((groups, node_dev, width), bf16),
        in_specs=[smem] * 3 + [hbm, [vmem] * len(banks), whole],
        out_specs=vmem,
        scratch_shapes=[
            pltpu.VMEM((groups * node_dev, width), f32),
            pltpu.VMEM((tile, width), bf16),
            pltpu.VMEM((slots, tile, tile), bf16),
            pltpu.SemaphoreType.DMA((slots,)),
        ],
        compiler_params=most,
        cost_estimate=pl.CostEstimate(
            flops=2 * slots * tile * tile * width, bytes_accessed=8 * 2**20, transcendentals=0
        ),
    )(tile_count, tile_pos, place, adj_tiles, list(banks), copies)
    return new_part[None], hidden, both[:width], both[width:], grad_bias


def solution(mesh):
    fine = Mesh(mesh.devices.reshape(SIZES), ALL)
    placed = (
        P(ALL, None, None),
        P(ALL),
        P(ALL),
        P(ALL, None),
        P(GRP, None, BLK, None),
        P(),
        P(),
        P(),
        P(ALL, None),
    )
    return jax.shard_map(
        body,
        mesh=fine,
        in_specs=placed,
        out_specs=(P(GRP, None, BLK, None), P(ALL, None), P(), P(), P()),
        check_vma=False,
    )
```

```python
import jax
import jax.numpy as jnp
from jax import lax
from jax.experimental import pallas as pl
from jax.experimental.pallas import tpu as pltpu
from jax.sharding import Mesh, PartitionSpec as P

GRP = ("y", "x_lo", "core")
PLANE = ("y", "x_lo", "core", "x_hi")
LINE = ("z_far", "z_mid", "z_near")
EVERY_OTHER = ("z_far", "z_mid")
BLK = ("x_hi",) + LINE
ALL = GRP + BLK
SIZES = (4, 2, 2, 2, 8, 2, 2)


def split_position(position, col_tiles, per_tile):
    return lax.div(position, col_tiles), lax.rem(position, col_tiles) * per_tile


def early_kernel(
    own_ref, stale_ref, feats_ref, w_self_ref, w_neigh_ref, cot_ref,
    sum_ref, base_ref, w_neigh_out, cot_out,
):
    groups = stale_ref.shape[0]
    own = own_ref[0]
    stale = jnp.zeros(sum_ref.shape, jnp.float32)
    for source in range(groups):
        keep = jnp.where(source == own, jnp.float32(0.0), jnp.float32(1.0))
        stale += stale_ref[source].astype(jnp.float32) * keep
    sum_ref[...] = stale
    preact = jnp.dot(feats_ref[...], w_self_ref[...], preferred_element_type=jnp.float32)
    base_ref[...] = preact
    w_neigh_out[...] = w_neigh_ref[...]
    cot_out[...] = cot_ref[...]


def layer_kernel(
    count_ref,
    pos_ref,
    place_ref,
    own_ref,
    adj_ref,
    bank_refs,
    stale_ref,
    base_ref,
    feats_ref,
    w_neigh_ref,
    bias_ref,
    cot_ref,
    hidden_ref,
    grads_ref,
    tiles_ref,
    sources_ref,
    tile_sem,
    source_sem,
):
    tile = adj_ref.shape[1]
    node_dev, width = stale_ref.shape
    per_tile = tile // node_dev
    bank_slots = 2 * bank_refs[0].shape[0]
    col_tiles = place_ref.shape[0] // per_tile
    own = own_ref[0]
    own_tile, own_part = lax.div(own, per_tile), lax.rem(own, per_tile)
    count = count_ref[0]

    def tile_copy(slot):
        rows = pl.ds(pl.multiple_of(own_part * node_dev, node_dev), node_dev)
        return pltpu.make_async_copy(
            adj_ref.at[slot, rows, :], tiles_ref.at[slot], tile_sem.at[slot]
        )

    def source_copy(slot, j, bank, block):
        return pltpu.make_async_copy(
            bank.at[block],
            sources_ref.at[slot, pl.ds(j * node_dev, node_dev), :],
            source_sem.at[slot, j],
        )

    def fetch(slot, carry):
        row_tile, first = split_position(pos_ref[slot], col_tiles, per_tile)

        @pl.when(row_tile == own_tile)
        def _():
            tile_copy(slot).start()
            for j in range(per_tile):
                place = place_ref[first + j]
                bank, block = lax.div(place, bank_slots), lax.rem(place, bank_slots)
                for choice, ref in enumerate(bank_refs):

                    @pl.when(bank == choice)
                    def _():
                        source_copy(slot, j, ref, block).start()

        return carry

    lax.fori_loop(0, count, fetch, 0)

    def add_tile(slot, fresh):
        row_tile, _ = split_position(pos_ref[slot], col_tiles, per_tile)

        def add():
            tile_copy(slot).wait()
            for j in range(per_tile):
                source_copy(slot, j, bank_refs[0], 0).wait()
            return fresh + jnp.dot(
                tiles_ref[slot], sources_ref[slot], preferred_element_type=jnp.float32
            )

        return lax.cond(row_tile == own_tile, add, lambda: fresh)

    fresh = lax.fori_loop(0, count, add_tile, jnp.zeros((node_dev, width), jnp.float32))
    aggregate = (fresh + stale_ref[...]).astype(jnp.bfloat16)
    feats = feats_ref[...]
    preact = base_ref[...]
    preact += jnp.dot(aggregate, w_neigh_ref[...], preferred_element_type=jnp.float32)
    preact += bias_ref[...]
    gate = jax.nn.sigmoid(preact)
    hidden_ref[...] = (preact * gate).astype(hidden_ref.dtype)
    grad_pre = (
        cot_ref[...].astype(jnp.float32) * gate * (1.0 + preact * (1.0 - gate))
    ).astype(jnp.bfloat16)
    both = jnp.concatenate([feats, aggregate], axis=1)
    grads = lax.dot_general(
        both, grad_pre, (((0,), (0,)), ((), ())), preferred_element_type=jnp.float32
    )
    bias_grad = jnp.sum(grad_pre.astype(jnp.float32), axis=0, keepdims=True)
    pieces, piece_rows, _ = grads_ref.shape
    hid = grads.shape[1]
    grads_ref[:, :, :hid] = grads.reshape(pieces, piece_rows, hid).astype(grads_ref.dtype)
    half = hid // 2
    tail = jnp.concatenate(
        [
            bias_grad[:, :half],
            bias_grad[:, half:],
            jnp.zeros((piece_rows - 2, half), jnp.float32),
        ],
        axis=0,
    )
    grads_ref[:, :, hid:] = jnp.broadcast_to(tail[None], (pieces, piece_rows, half)).astype(
        grads_ref.dtype
    )


def partial_kernel(
    count_ref,
    pos_ref,
    place_ref,
    adj_ref,
    bank_refs,
    _,
    part_ref,
    acc_ref,
    source_ref,
    tiles_ref,
    tile_sem,
):
    tile = adj_ref.shape[1]
    _, node_dev, _ = part_ref.shape
    per_tile = tile // node_dev
    bank_slots = 2 * bank_refs[0].shape[0]
    col_tiles = place_ref.shape[0] // per_tile
    count = count_ref[0]

    def tile_copy(slot):
        return pltpu.make_async_copy(adj_ref.at[slot], tiles_ref.at[slot], tile_sem.at[slot])

    def fetch(slot, carry):
        tile_copy(slot).start()
        return carry

    lax.fori_loop(0, count, fetch, 0)
    acc_ref[...] = jnp.zeros_like(acc_ref)

    def add_tile(slot, carry):
        row_tile, first = split_position(pos_ref[slot], col_tiles, per_tile)
        for j in range(per_tile):
            place = place_ref[first + j]
            bank, block = lax.div(place, bank_slots), lax.rem(place, bank_slots)
            for choice, ref in enumerate(bank_refs):

                @pl.when(bank == choice)
                def _():
                    source_ref[j * node_dev : (j + 1) * node_dev, :] = ref[block]

        tile_copy(slot).wait()
        product = jnp.dot(tiles_ref[slot], source_ref[...], preferred_element_type=jnp.float32)
        rows = pl.ds(pl.multiple_of(row_tile * tile, tile), tile)
        acc_ref[rows, :] += product
        return carry

    lax.fori_loop(0, count, add_tile, 0)
    part_ref[...] = acc_ref[...].reshape(part_ref.shape).astype(part_ref.dtype)


def finish_kernel(got_ref, self_ref, neigh_ref, bias_ref):
    pairs, rows, _ = got_ref.shape
    width, hid = self_ref.shape
    got = got_ref[...].astype(jnp.float32).reshape(pairs // 2, 2, rows, got_ref.shape[2])
    total = got[:, 0] + got[:, 1]
    both = total[:, :, :hid].reshape(2 * width, hid)
    self_ref[...] = both[:width]
    neigh_ref[...] = both[width:]
    half = hid // 2
    bias_ref[:, :half] = total[0, 0:1, hid:]
    bias_ref[:, half:] = total[0, 1:2, hid:]


def body(
    adj_tiles, tile_pos, tile_count, node_feats, stale_part, w_self, w_neigh, bias_vec, cotangent
):
    node_dev, width = node_feats.shape
    hid = cotangent.shape[1]
    groups = lax.axis_size(GRP)
    blocks = lax.axis_size(BLK)
    plane = lax.axis_size(PLANE)

    stale = lax.all_to_all(stale_part[0], GRP, 0, 0, tiled=True)
    same = lax.all_gather(node_feats, EVERY_OTHER)
    length = lax.axis_size(LINE)
    up = [(i, (i + 1) % length) for i in range(length)]
    down = [(i, (i - 1) % length) for i in range(length)]
    cut = same.shape[0] // 2
    low, high = same[:cut], same[cut:]
    swap = [(0, 1), (1, 0)]
    side_low, side_high = lax.ppermute(low, "x_hi", swap), lax.ppermute(high, "x_hi", swap)
    beside = lax.ppermute(same, LINE, up)
    banks = (
        same,
        beside,
        side_low,
        side_high,
        lax.ppermute(side_low, LINE, down),
        lax.ppermute(side_high, LINE, up),
    )
    index = jnp.arange(blocks, dtype=jnp.int32)
    other_side = index // length != lax.axis_index("x_hi")
    other_parity = index % 2 != lax.axis_index("z_near")
    slot = index % length // 2
    low_bank = jnp.where(other_side, 2 + 2 * other_parity, other_parity)
    first = other_side & (slot >= cut)
    place = (low_bank + first) * length + jnp.where(first, slot - cut, slot)
    own = lax.axis_index(GRP).reshape(1).astype(jnp.int32)

    smem = pl.BlockSpec(memory_space=pltpu.SMEM)
    vmem = pl.BlockSpec(memory_space=pltpu.VMEM)
    piece_rows = 2 * width // plane
    tile, slots = adj_tiles.shape[1], adj_tiles.shape[0]
    whole = pl.BlockSpec(memory_space=pl.ANY)
    hbm = pl.BlockSpec(memory_space=pltpu.HBM)
    bf16, f32 = jnp.bfloat16, jnp.float32
    limit = pltpu.CompilerParams(vmem_limit_bytes=32 * 1024 * 1024)
    broad = pltpu.CompilerParams(vmem_limit_bytes=51 * 1024 * 1024)
    most = pltpu.CompilerParams(vmem_limit_bytes=62 * 1024 * 1024)
    stale_sum, base, w_neigh, cotangent = pl.pallas_call(
        early_kernel,
        out_shape=(
            jax.ShapeDtypeStruct((node_dev, width), f32),
            jax.ShapeDtypeStruct((node_dev, hid), f32),
            jax.ShapeDtypeStruct(w_neigh.shape, bf16),
            jax.ShapeDtypeStruct(cotangent.shape, bf16),
        ),
        in_specs=[smem] + [vmem] * 5,
        out_specs=(vmem,) * 4,
        compiler_params=limit,
        cost_estimate=pl.CostEstimate(
            flops=2 * node_dev * width * hid, bytes_accessed=2**20, transcendentals=0
        ),
    )(own, stale, node_feats, w_self, w_neigh, cotangent)
    hidden, grads = pl.pallas_call(
        layer_kernel,
        out_shape=(
            jax.ShapeDtypeStruct((node_dev, hid), bf16),
            jax.ShapeDtypeStruct((plane, piece_rows, hid + hid // 2), bf16),
        ),
        in_specs=[smem] * 4 + [hbm, [whole] * len(banks)] + [vmem] * 6,
        out_specs=(vmem, vmem),
        scratch_shapes=[
            pltpu.VMEM((slots, node_dev, tile), bf16),
            pltpu.VMEM((slots, tile, width), bf16),
            pltpu.SemaphoreType.DMA((slots,)),
            pltpu.SemaphoreType.DMA((slots, tile // node_dev)),
        ],
        compiler_params=broad,
        cost_estimate=pl.CostEstimate(
            flops=8 * node_dev * width * hid, bytes_accessed=2**20, transcendentals=0
        ),
    )(
        tile_count,
        tile_pos,
        place,
        own,
        adj_tiles,
        list(banks),
        stale_sum,
        base,
        node_feats,
        w_neigh,
        bias_vec[None],
        cotangent,
    )
    scaling = float(node_dev * groups * blocks) ** (-0.5)
    piece = lax.all_to_all(grads, PLANE, 0, 0, tiled=True).astype(f32)
    piece = lax.all_gather(jnp.sum(piece, axis=0).astype(bf16), EVERY_OTHER).astype(f32)
    piece = (jnp.sum(piece, axis=0) * scaling).astype(bf16)
    pair = plane * lax.axis_size("z_near")
    copies = jnp.broadcast_to(piece[None], (pair,) + piece.shape)
    got = lax.all_to_all(copies, PLANE + ("z_near",), 0, 0, tiled=True)
    grad_self, grad_neigh, grad_bias = pl.pallas_call(
        finish_kernel,
        out_shape=(
            jax.ShapeDtypeStruct((width, hid), f32),
            jax.ShapeDtypeStruct((width, hid), f32),
            jax.ShapeDtypeStruct((1, hid), f32),
        ),
        in_specs=[vmem],
        out_specs=(vmem,) * 3,
        compiler_params=limit,
    )(got)
    new_part = pl.pallas_call(
        partial_kernel,
        out_shape=jax.ShapeDtypeStruct((groups, node_dev, width), bf16),
        in_specs=[smem] * 3 + [hbm, [vmem] * len(banks), whole],
        out_specs=vmem,
        scratch_shapes=[
            pltpu.VMEM((groups * node_dev, width), f32),
            pltpu.VMEM((tile, width), bf16),
            pltpu.VMEM((slots, tile, tile), bf16),
            pltpu.SemaphoreType.DMA((slots,)),
        ],
        compiler_params=most,
        cost_estimate=pl.CostEstimate(
            flops=2 * slots * tile * tile * width, bytes_accessed=8 * 2**20, transcendentals=0
        ),
    )(tile_count, tile_pos, place, adj_tiles, list(banks), copies)
    return new_part[None], hidden, grad_self, grad_neigh, grad_bias.reshape(hid)


def solution(mesh):
    fine = Mesh(mesh.devices.reshape(SIZES), ALL)
    placed = (
        P(ALL, None, None),
        P(ALL),
        P(ALL),
        P(ALL, None),
        P(GRP, None, BLK, None),
        P(),
        P(),
        P(),
        P(ALL, None),
    )
    return jax.shard_map(
        body,
        mesh=fine,
        in_specs=placed,
        out_specs=(P(GRP, None, BLK, None), P(ALL, None), P(), P(), P()),
        check_vma=False,
    )
```
